32 devices in a mesh: pipe: 2 (over core), dp: 4 (over z), tensor: 4 (over y, x).
Axes of the slice: x: 2, y: 2, z: 4, core: 2. Of those that a mesh axis runs over, the one named last changes fastest.
Arguments:
- stream_in: bfloat16 [2, 2048, 4096], P('pipe', 'dp', 'tensor'), may hold values from -4.5 to 4.5
- saved_in: bfloat16 [2, 2048, 4096], P('pipe', 'dp', 'tensor'), may hold values from -4.5 to 4.5
- grad_out: bfloat16 [2, 2048, 4096], P('pipe', 'dp', 'tensor'), may hold values from -6 to 6
- mem_keys: bfloat16 [2, 8, 8, 4096], P('pipe', 'dp', None, 'tensor'), may hold values from -4.5 to 4.5
- mem_values: bfloat16 [2, 8, 8, 4096], P('pipe', 'dp', None, 'tensor'), may hold values from -6 to 6
- owner_map: int32 [8], replicated, may hold values from 0 to 7, as said below
- block_ids: int32 [2, 2, 4, 1], P(None, 'pipe', 'dp'), may hold values from 0 to 7, as said below
Outputs:
- next_input: bfloat16 [2, 2048, 4096], P('pipe', 'dp', 'tensor')
- grad_back: bfloat16 [2, 2048, 4096], P('pipe', 'dp', 'tensor')
- key_grad: bfloat16 [2, 8, 8, 4096], P('pipe', 'dp', None, 'tensor')
- value_grad: bfloat16 [2, 8, 8, 4096], P('pipe', 'dp', None, 'tensor')
The draws below stay inside these ranges and needn't reach their ends.
Inputs may be any that keep to these rules, and one draw needn't show every extreme that they name: `owner_map`: A permutation of the block ids; location loc lies with replica loc // 2 in slot loc % 2. `block_ids`: for each section and replica, the 2 ids of both micro-batches together lie with 2 different replicas, so at most one block is requested from one replica; in every section one replica is asked for a block by every replica, itself included.
All inputs are finite; a program needn't handle non-finite values.
Results may differ from the reference program's by a relative error of at most 0.0057.
Values may be sent and summed in bfloat16 or wider, within the bound.
No kernel may reach another device: no remote copies, remote signals or barrier semaphores. Data moves between devices by JAX's collectives and lax.ppermute only.
A program may use at most 64 MiB of HBM per device.

```python
import math
import jax
import jax.numpy as jnp
from jax import lax

HEAD_DIM = 128
MEM_BLK = 8
TOK_DEV = 512
MB_DEV = 2
TOPK = 1
SECTIONS = 2
TOKENS = 2048
FEATURES = 4096
MEM_BLOCKS = 8
N_DP = 4


def activation(key, code):
    local = jax.random.fold_in(key, code)
    shape = (SECTIONS, TOKENS, FEATURES)
    result = jnp.clip(jax.random.normal(local, shape, jnp.float32), -4.5, 4.5)
    return result.astype(jnp.bfloat16)


def draw_stream_in(key, part):
    return activation(key, 1)


def draw_saved_in(key, part):
    return activation(key, 2)


def draw_mem_keys(key, part):
    local = jax.random.fold_in(key, 3)
    shape = (SECTIONS, MEM_BLOCKS, MEM_BLK, FEATURES)
    result = jnp.clip(jax.random.normal(local, shape, jnp.float32), -4.5, 4.5)
    return result.astype(jnp.bfloat16)


def shared_tables(key):
    base = jax.random.fold_in(key, 5)
    owner_map = jax.random.permutation(jax.random.fold_in(base, 0), MEM_BLOCKS).astype(jnp.int32)
    holder = jnp.argsort(owner_map).astype(jnp.int32)
    replicas = MEM_BLOCKS // MB_DEV
    total_rows = SECTIONS * replicas
    row_keys = jax.random.split(jax.random.fold_in(base, 1), total_rows)
    hot = jax.random.randint(jax.random.fold_in(base, 3), (SECTIONS,), 0, replicas).astype(jnp.int32)
    hot_rows = jnp.repeat(hot, replicas)

    def pick_row(row_key, hot_one):
        others = jax.random.permutation(row_key, replicas - 1)[:2 * TOPK - 1].astype(jnp.int32)
        others = others + (others >= hot_one).astype(jnp.int32)
        members = jnp.concatenate([hot_one[None], others])
        order = jax.random.permutation(jax.random.fold_in(row_key, 7), 2 * TOPK)
        return members[order].astype(jnp.int32)
    chosen = jax.vmap(pick_row)(row_keys, hot_rows)
    slot_ids = jax.random.randint(jax.random.fold_in(base, 2), (total_rows, 2 * TOPK), 0, MB_DEV)
    places = (chosen * MB_DEV + slot_ids).astype(jnp.int32)
    picked = holder[places].reshape(SECTIONS, replicas, 2, TOPK)
    return (owner_map, jnp.transpose(picked, (2, 0, 1, 3)).astype(jnp.int32))


def draw_owner_map(key, part):
    return shared_tables(key)[0]


def draw_block_ids(key, part):
    return shared_tables(key)[1]


def block_levels(own_key, shape, cuts, least, top_value):
    loudness, own = 1.0, jax.random.fold_in(own_key, 6)
    for axis_at, shards_of in cuts:
        draws = jnp.exp(jax.random.uniform(jax.random.fold_in(own, axis_at), (shards_of,), jnp.float32, least / len(cuts), top_value / len(cuts)))
        loudness = loudness * jnp.repeat(draws, shape[axis_at] // shards_of).reshape([-1 if axis == axis_at else 1 for axis in range(len(shape))])
    return loudness


def bell_draw(stream_key, extent, deviation, limit, cuts=(), dtype=jnp.bfloat16):
    values = jax.random.normal(stream_key, extent, jnp.float32) * deviation
    if len(cuts) > 0:
        values = block_levels(stream_key, extent, cuts, -0.22, 0.18) * values
    return jnp.clip(values, min=-limit, max=limit).astype(dtype)


def setup_inputs(seed: int = 0) -> dict:
    arg_keys = jax.random.split(jax.random.key(seed), 8)
    return {
        "stream_in": draw_stream_in(jax.random.fold_in(arg_keys[7], 71), 0),
        "saved_in": draw_saved_in(jax.random.fold_in(arg_keys[7], 71), 0),
        "grad_out": bell_draw(arg_keys[2], (SECTIONS, TOKENS, FEATURES), 1.0, 6.0, ((0, 2), (1, 4), (2, 4))),
        "mem_keys": draw_mem_keys(jax.random.fold_in(arg_keys[7], 71), 0),
        "mem_values": bell_draw(arg_keys[4], (SECTIONS, MEM_BLOCKS, MEM_BLK, FEATURES), 1.0, 6.0, ((0, 2), (1, 4), (3, 4))),
        "owner_map": draw_owner_map(jax.random.fold_in(arg_keys[7], 71), 0),
        "block_ids": draw_block_ids(jax.random.fold_in(arg_keys[7], 71), 0),
    }


def forward_part(inputs, memory_keys, memory_values):
    rows = inputs.shape[0]
    heads_count = inputs.shape[1] // HEAD_DIM
    scale = 1.0 / math.sqrt(HEAD_DIM)
    queries = inputs.astype(jnp.float32).reshape(rows, heads_count, HEAD_DIM)
    key_rows = memory_keys.astype(jnp.float32).reshape(-1, heads_count, HEAD_DIM)
    value_rows = memory_values.astype(jnp.float32).reshape(-1, heads_count, HEAD_DIM)
    scores = jnp.einsum('thd,khd->htk', queries, key_rows) * scale
    exponent = jnp.exp(scores - lax.optimization_barrier(jnp.max(scores, axis=-1, keepdims=True)))
    weights = exponent / lax.optimization_barrier(jnp.sum(exponent, axis=-1, keepdims=True))
    rounded = lax.optimization_barrier(weights.astype(jnp.bfloat16)).astype(jnp.float32)
    attended = jnp.einsum('htk,khd->thd', rounded, value_rows).reshape(rows, -1)
    return (queries, key_rows, value_rows, weights, rounded, attended)

def backward_part(inputs, grads, memory_keys, memory_values):
    queries, key_rows, value_rows, weights, rounded, attended = forward_part(inputs, memory_keys, memory_values)
    rows = inputs.shape[0]
    heads_count = queries.shape[1]
    scale = 1.0 / math.sqrt(HEAD_DIM)
    grad_rows = grads.astype(jnp.float32).reshape(rows, heads_count, HEAD_DIM)
    grad_weights = jnp.einsum('thd,khd->htk', grad_rows, value_rows)
    centre = lax.optimization_barrier(jnp.sum(weights * grad_weights, axis=-1, keepdims=True))
    grad_scores = weights * (grad_weights - centre) * scale
    grad_scores = lax.optimization_barrier(grad_scores.astype(jnp.bfloat16)).astype(jnp.float32)
    grad_queries = jnp.einsum('htk,khd->thd', grad_scores, key_rows).reshape(rows, -1)
    key_terms = jnp.einsum('htk,thd->khd', grad_scores, queries).reshape(key_rows.shape[0], -1)
    value_terms = jnp.einsum('htk,thd->khd', rounded, grad_rows).reshape(key_rows.shape[0], -1)
    input_grad = (grads.astype(jnp.float32) + grad_queries).astype(jnp.bfloat16)
    return (input_grad, key_terms.astype(jnp.bfloat16), value_terms.astype(jnp.bfloat16))

def reference(stream_in, saved_in, grad_out, mem_keys, mem_values, owner_map, block_ids):
    locations = owner_map[block_ids].astype(jnp.int32)
    width = stream_in.shape[2]

    def section(packed):
        forward_rows, backward_rows, upstream, sec_keys, sec_values, places = packed

        def fetch(where):
            return (sec_keys[where].reshape(TOPK * MEM_BLK, width), sec_values[where].reshape(TOPK * MEM_BLK, width))

        def forward_one(inputs, where):
            fetched_keys, fetched_values = fetch(where)
            attended = forward_part(inputs, fetched_keys, fetched_values)[5]
            return (inputs.astype(jnp.float32) + attended).astype(jnp.bfloat16)

        def backward_one(inputs, grads, where):
            fetched_keys, fetched_values = fetch(where)
            return backward_part(inputs, grads, fetched_keys, fetched_values)
        outputs = jax.vmap(forward_one)(forward_rows.reshape(N_DP, TOK_DEV, width), places[0])
        input_grads, key_terms, value_terms = jax.vmap(backward_one)(backward_rows.reshape(N_DP, TOK_DEV, width), upstream.reshape(N_DP, TOK_DEV, width), places[1])
        flat = places[1].reshape(-1)
        key_total = jnp.zeros((MEM_BLOCKS, MEM_BLK, width), jnp.float32).at[flat].add(key_terms.astype(jnp.float32).reshape(N_DP * TOPK, MEM_BLK, width))
        value_total = jnp.zeros((MEM_BLOCKS, MEM_BLK, width), jnp.float32).at[flat].add(value_terms.astype(jnp.float32).reshape(N_DP * TOPK, MEM_BLK, width))
        return (outputs.reshape(TOKENS, width), input_grads.reshape(TOKENS, width), key_total.astype(jnp.bfloat16), value_total.astype(jnp.bfloat16))
    results = lax.map(section, (stream_in, saved_in, grad_out, mem_keys, mem_values, jnp.moveaxis(locations, 1, 0)))
    blank = jnp.zeros((1, TOKENS, width), jnp.bfloat16)
    next_input = jnp.concatenate([blank, results[0][:-1]], axis=0)
    grad_back = jnp.concatenate([results[1][1:], blank], axis=0)
    return (next_input, grad_back, results[2], results[3])
```

```python
import functools
import math

import jax
import jax.numpy as jnp
from jax import lax
from jax.experimental import pallas as pl
from jax.experimental.pallas import tpu as pltpu
from jax.sharding import PartitionSpec as P

HEAD_DIM = 128
DIRECT_REPLICAS = 8
VMEM = pl.BlockSpec(memory_space=pltpu.VMEM)
SMEM = pl.BlockSpec(memory_space=pltpu.SMEM)
NT = (((1,), (1,)), ((), ()))
NN = (((1,), (0,)), ((), ()))
TN = (((0,), (0,)), ((), ()))


def dot(a, b, dims):
    return lax.dot_general(a, b, dims, preferred_element_type=jnp.float32)


def by_head(block):
    keys, width = block.shape
    heads = width // HEAD_DIM
    wide = jnp.broadcast_to(block.astype(jnp.float32)[None], (heads, keys, width))
    head = lax.broadcasted_iota(jnp.int32, wide.shape, 0)
    feature_head = lax.broadcasted_iota(jnp.int32, wide.shape, 2) // HEAD_DIM
    return jnp.where(head == feature_head, wide, 0.0).reshape(heads * keys, width).astype(block.dtype)


def own_head(product, keys):
    heads = product.shape[0] // keys
    parts = [
        product[h * keys : (h + 1) * keys, h * HEAD_DIM : (h + 1) * HEAD_DIM] for h in range(heads)
    ]
    return jnp.concatenate(parts, axis=1)


def softmax_t(keys_by_head, rows, heads):
    scores = dot(keys_by_head, rows, NT) * (1.0 / math.sqrt(HEAD_DIM))
    scores = scores.reshape(heads, -1, rows.shape[0])
    exponent = jnp.exp(scores - jnp.max(scores, axis=1, keepdims=True))
    return exponent / jnp.sum(exponent, axis=1, keepdims=True)


def pick(refs, owner, slot, me, replicas):
    behind = lax.rem(me - owner + replicas, replicas)
    block = refs[0][slot]
    for d in range(1, replicas):
        block = jnp.where(behind == d, refs[d][slot], block)
    return block


def score_kernel(replicas, slots, *refs):
    map_ref, ids_ref, stream_ref, saved_ref, grad_ref = refs[:5]
    key_refs, value_refs = refs[5 : 5 + replicas], refs[5 + replicas : 5 + 2 * replicas]
    terms_ref, weights_ref, block_ref = refs[5 + 2 * replicas :]
    me = lax.axis_index("dp")
    width = stream_ref.shape[1]
    heads = width // HEAD_DIM
    back = map_ref[ids_ref[1]]
    owner, slot = back // slots, back % slots
    keys = pick(key_refs, owner, slot, me, replicas)
    values = pick(value_refs, owner, slot, me, replicas)
    count = keys.shape[0]
    saved, grads = saved_ref[...], grad_ref[...]
    weights = softmax_t(by_head(keys), saved, heads)
    grad_weights = dot(by_head(values), grads, NT).reshape(weights.shape)
    centre = jnp.sum(weights * grad_weights, axis=1, keepdims=True)
    grad_scores = weights * (grad_weights - centre) * (1.0 / math.sqrt(HEAD_DIM))
    flat = (heads * count, saved.shape[0])
    grad_scores = grad_scores.astype(jnp.bfloat16).reshape(flat)
    rounded = weights.astype(jnp.bfloat16).reshape(flat)
    terms_ref[:, :width] = own_head(dot(grad_scores, saved, NN), count).astype(jnp.bfloat16)
    terms_ref[:, width : 2 * width] = own_head(dot(rounded, grads, NN), count).astype(jnp.bfloat16)
    place = jnp.full((count, HEAD_DIM), back, jnp.int32)
    terms_ref[:, 2 * width :] = place.astype(jnp.float32).astype(jnp.bfloat16)
    section = lax.axis_index("pipe")

    @pl.when(section == 0)
    def _():
        ahead = map_ref[ids_ref[0]]
        owner, slot = ahead // slots, ahead % slots
        first = by_head(pick(key_refs, owner, slot, me, replicas))
        block_ref[...] = pick(value_refs, owner, slot, me, replicas)
        wide = softmax_t(first, stream_ref[...], heads)
        weights_ref[...] = wide.astype(jnp.bfloat16).reshape(flat)

    @pl.when(section != 0)
    def _():
        weights_ref[...] = grad_scores
        block_ref[...] = keys


def output_kernel(rows_ref, weights_ref, block_ref, next_ref, back_ref):
    section = lax.axis_index("pipe")
    added = dot(weights_ref[...], by_head(block_ref[...]), TN)
    out = (rows_ref[...].astype(jnp.float32) + added).astype(jnp.bfloat16)
    blank = jnp.zeros_like(out)
    next_ref[...] = jnp.where(section == 0, blank, out)
    back_ref[...] = jnp.where(section == 0, out, blank)


def sum_kernel(replicas, slots, *refs):
    terms_refs, (key_ref, value_ref) = refs[:replicas], refs[replicas:]
    me = lax.axis_index("dp")
    width = key_ref.shape[2]
    tiles = width // HEAD_DIM
    terms = [ref[...].astype(jnp.float32) for ref in terms_refs]
    for slot in range(slots):
        here = (me * slots + slot).astype(jnp.float32)
        hits = [t[:, 2 * width :] == here for t in terms]
        for i in range(2 * tiles):
            at = slice(i * HEAD_DIM, (i + 1) * HEAD_DIM)
            total = sum(jnp.where(hit, t[:, at], 0.0) for hit, t in zip(hits, terms))
            out, j = (key_ref, i) if i < tiles else (value_ref, i - tiles)
            out[slot, :, j * HEAD_DIM : (j + 1) * HEAD_DIM] = total.astype(jnp.bfloat16)


def around(x, replicas):
    return [x] + [
        lax.ppermute(x, "dp", [(i, (i + d) % replicas) for i in range(replicas)])
        for d in range(1, replicas)
    ]


def direct(stream_in, saved_in, grad_out, mem_keys, mem_values, owner_map, block_ids):
    replicas = lax.axis_size("dp")
    slots, block_rows, width = mem_keys.shape[1:]
    rows = stream_in.shape[1]
    heads = width // HEAD_DIM
    swap = [(0, 1), (1, 0)]
    key_parts = around(mem_keys[0], replicas)
    value_parts = around(mem_values[0], replicas)
    section = lax.axis_index("pipe")
    sent = jnp.where(section == 0, stream_in[0], grad_out[0])
    other_rows = lax.ppermute(sent, "pipe", swap)
    terms, weights, block = pl.pallas_call(
        functools.partial(score_kernel, replicas, slots),
        out_shape=(
            jax.ShapeDtypeStruct((block_rows, 2 * width + HEAD_DIM), jnp.bfloat16),
            jax.ShapeDtypeStruct((heads * block_rows, rows), jnp.bfloat16),
            jax.ShapeDtypeStruct((block_rows, width), jnp.bfloat16),
        ),
        in_specs=[SMEM] * 2 + [VMEM] * (3 + 2 * replicas),
        out_specs=(VMEM,) * 3,
        name="scores",
    )(owner_map, block_ids.reshape(-1), stream_in[0], saved_in[0], grad_out[0], *key_parts, *value_parts)
    term_parts = around(terms, replicas)
    other_weights = lax.ppermute(weights, "pipe", swap)
    other_block = lax.ppermute(block, "pipe", swap)
    next_input, grad_back = pl.pallas_call(
        output_kernel,
        out_shape=(jax.ShapeDtypeStruct((rows, width), jnp.bfloat16),) * 2,
        in_specs=[VMEM] * 3,
        out_specs=(VMEM,) * 2,
        cost_estimate=pl.CostEstimate(flops=2 * 256 * rows * width, bytes_accessed=6 * rows * width, transcendentals=0),
        name="outputs",
    )(other_rows, other_weights, other_block)
    key_grad, value_grad = pl.pallas_call(
        functools.partial(sum_kernel, replicas, slots),
        out_shape=(jax.ShapeDtypeStruct((slots, block_rows, width), jnp.bfloat16),) * 2,
        in_specs=[VMEM] * replicas,
        out_specs=(VMEM,) * 2,
        name="sums",
    )(*term_parts)
    return next_input[None], grad_back[None], key_grad[None], value_grad[None]


def from_behind(x, axis, by):
    peers = lax.axis_size(axis)
    pairs = [(i, i + by) for i in range(peers) if 0 <= i + by < peers]
    return lax.ppermute(x, axis, pairs)


def forward_part(inputs, memory_keys, memory_values):
    rows = inputs.shape[0]
    heads_count = inputs.shape[1] // HEAD_DIM
    scale = 1.0 / math.sqrt(HEAD_DIM)
    queries = inputs.reshape(rows, heads_count, HEAD_DIM)
    key_rows = memory_keys.reshape(-1, heads_count, HEAD_DIM)
    value_rows = memory_values.reshape(-1, heads_count, HEAD_DIM)
    scores = (
        jnp.einsum("thd,khd->htk", queries, key_rows, preferred_element_type=jnp.float32) * scale
    )
    exponent = jnp.exp(scores - jnp.max(scores, axis=-1, keepdims=True))
    weights = exponent / jnp.sum(exponent, axis=-1, keepdims=True)
    rounded = weights.astype(jnp.bfloat16)
    attended = jnp.einsum(
        "htk,khd->thd", rounded, value_rows, preferred_element_type=jnp.float32
    ).reshape(rows, -1)
    return (queries, key_rows, value_rows, weights, rounded, attended)


def backward_part(inputs, grads, memory_keys, memory_values):
    queries, key_rows, value_rows, weights, rounded, attended = forward_part(
        inputs, memory_keys, memory_values
    )
    rows = inputs.shape[0]
    heads_count = queries.shape[1]
    scale = 1.0 / math.sqrt(HEAD_DIM)
    grad_rows = grads.reshape(rows, heads_count, HEAD_DIM)
    grad_weights = jnp.einsum(
        "thd,khd->htk", grad_rows, value_rows, preferred_element_type=jnp.float32
    )
    centre = jnp.sum(weights * grad_weights, axis=-1, keepdims=True)
    grad_scores = (weights * (grad_weights - centre) * scale).astype(jnp.bfloat16)
    grad_queries = jnp.einsum(
        "htk,khd->thd", grad_scores, key_rows, preferred_element_type=jnp.float32
    ).reshape(rows, -1)
    key_terms = jnp.einsum("htk,thd->khd", grad_scores, queries, preferred_element_type=jnp.float32)
    value_terms = jnp.einsum("htk,thd->khd", rounded, grad_rows, preferred_element_type=jnp.float32)
    input_grad = (grads.astype(jnp.float32) + grad_queries).astype(jnp.bfloat16)
    key_count = key_rows.shape[0]
    return (
        input_grad,
        key_terms.reshape(key_count, -1).astype(jnp.bfloat16),
        value_terms.reshape(key_count, -1).astype(jnp.bfloat16),
    )


def routed(stream_in, saved_in, grad_out, mem_keys, mem_values, owner_map, block_ids):
    replicas = lax.axis_size("dp")
    local_blocks = mem_keys.shape[1]
    block_rows = mem_keys.shape[2]
    width = stream_in.shape[2]
    table_size = owner_map.shape[0]
    requested = block_ids.reshape(-1)
    picks = requested.shape[0]
    half = picks // 2
    matches = requested[:, None] == jnp.arange(table_size, dtype=jnp.int32)[None, :]
    places = jnp.sum(jnp.where(matches, owner_map[None, :], 0), axis=1)
    owners = places // local_blocks
    slot_ids = places % local_blocks
    owner_hits = owners[:, None] == jnp.arange(replicas, dtype=jnp.int32)[None, :]
    served = None
    wanted = jnp.sum(jnp.where(owner_hits, slot_ids[:, None], 0), axis=0)
    served = lax.all_to_all(
        wanted.reshape(replicas, 1), "dp", split_axis=0, concat_axis=0, tiled=True
    ).reshape(replicas)
    out_keys = jnp.take(mem_keys[0], served, axis=0)
    out_values = jnp.take(mem_values[0], served, axis=0)
    got_keys, got_values = (
        lax.all_to_all(out_keys, "dp", split_axis=0, concat_axis=0, tiled=True),
        lax.all_to_all(out_values, "dp", split_axis=0, concat_axis=0, tiled=True),
    )
    fetched_keys = jnp.take(got_keys, owners, axis=0)
    fetched_values = jnp.take(got_values, owners, axis=0)
    forward_keys = fetched_keys[:half].reshape(-1, width)
    forward_values = fetched_values[:half].reshape(-1, width)
    backward_keys = fetched_keys[half:].reshape(-1, width)
    backward_values = fetched_values[half:].reshape(-1, width)
    attended = forward_part(stream_in[0], forward_keys, forward_values)[5]
    section_out = (stream_in[0].astype(jnp.float32) + attended).astype(jnp.bfloat16)
    next_input = from_behind(section_out[None], "pipe", 1)
    input_grad, key_terms, value_terms = backward_part(
        saved_in[0], grad_out[0], backward_keys, backward_values
    )
    grad_back = from_behind(input_grad[None], "pipe", -1)
    key_blocks = key_terms.reshape(half, block_rows, width)
    value_blocks = value_terms.reshape(half, block_rows, width)
    back_hits = owner_hits[half:].astype(jnp.bfloat16)
    send_keys = jnp.einsum(
        "ro,rtf->otf", back_hits, key_blocks, preferred_element_type=jnp.float32
    ).astype(jnp.bfloat16)
    send_values = jnp.einsum(
        "ro,rtf->otf", back_hits, value_blocks, preferred_element_type=jnp.float32
    ).astype(jnp.bfloat16)
    recv_keys, recv_values = (
        lax.all_to_all(send_keys, "dp", split_axis=0, concat_axis=0, tiled=True),
        lax.all_to_all(send_values, "dp", split_axis=0, concat_axis=0, tiled=True),
    )
    slot_hits = (served[:, None] == jnp.arange(local_blocks, dtype=jnp.int32)[None, :]).astype(
        jnp.bfloat16
    )
    key_grad = jnp.einsum(
        "sm,stf->mtf", slot_hits, recv_keys, preferred_element_type=jnp.float32
    ).astype(jnp.bfloat16)
    value_grad = jnp.einsum(
        "sm,stf->mtf", slot_hits, recv_values, preferred_element_type=jnp.float32
    ).astype(jnp.bfloat16)
    return (next_input, grad_back, key_grad[None], value_grad[None])


def local(*args):
    one_each = args[-1].size == 2 and lax.axis_size("pipe") == 2
    plan = direct if one_each and lax.axis_size("dp") <= DIRECT_REPLICAS else routed
    return plan(*args)


def solution(mesh):
    in_specs = (
        P("pipe", "dp", "tensor"),
        P("pipe", "dp", "tensor"),
        P("pipe", "dp", "tensor"),
        P("pipe", "dp", None, "tensor"),
        P("pipe", "dp", None, "tensor"),
        P(),
        P(None, "pipe", "dp", None),
    )
    out_specs = (
        P("pipe", "dp", "tensor"),
        P("pipe", "dp", "tensor"),
        P("pipe", "dp", None, "tensor"),
        P("pipe", "dp", None, "tensor"),
    )
    return jax.shard_map(local, mesh=mesh, in_specs=in_specs, out_specs=out_specs, check_vma=False)
```

```python
import functools
import math

import jax
import jax.numpy as jnp
from jax import lax
from jax.experimental import pallas as pl
from jax.experimental.pallas import tpu as pltpu
from jax.sharding import PartitionSpec as P

HEAD_DIM = 128
DIRECT_REPLICAS = 8
FETCH_ORDER = (2, 3, 1)
SEND_ORDER = (1, 3, 2)
HBM = pl.BlockSpec(memory_space=pltpu.HBM)
VMEM = pl.BlockSpec(memory_space=pltpu.VMEM)
SMEM = pl.BlockSpec(memory_space=pltpu.SMEM)
NT = (((1,), (1,)), ((), ()))
NN = (((1,), (0,)), ((), ()))
TN = (((0,), (0,)), ((), ()))


def padded(rows):
    return -(-rows // 16) * 16


def dot(a, b, dims):
    return lax.dot_general(a, b, dims, preferred_element_type=jnp.float32)


def by_head(block):
    keys, width = block.shape
    heads = width // HEAD_DIM
    wide = jnp.broadcast_to(block.astype(jnp.float32)[None], (heads, keys, width))
    head = lax.broadcasted_iota(jnp.int32, wide.shape, 0)
    feature_head = lax.broadcasted_iota(jnp.int32, wide.shape, 2) // HEAD_DIM
    return jnp.where(head == feature_head, wide, 0.0).reshape(heads * keys, width).astype(block.dtype)


def own_head(product, keys):
    heads = product.shape[0] // keys
    parts = [
        product[h * keys : (h + 1) * keys, h * HEAD_DIM : (h + 1) * HEAD_DIM] for h in range(heads)
    ]
    return jnp.concatenate(parts, axis=1)


def softmax_t(keys_by_head, rows, heads):
    scores = dot(keys_by_head, rows, NT) * (1.0 / math.sqrt(HEAD_DIM))
    scores = scores.reshape(heads, -1, rows.shape[0])
    exponent = jnp.exp(scores - jnp.max(scores, axis=1, keepdims=True))
    return exponent / jnp.sum(exponent, axis=1, keepdims=True)


def pick(refs, first, owner, slot, me):
    block = refs[0][first + slot]
    for d in range(1, len(refs)):
        block = jnp.where(owner == me ^ d, refs[d][first + slot], block)
    return block


def stack_kernel(keys_ref, values_ref, out_ref, sems):
    slots = keys_ref.shape[0]
    copies = [
        pltpu.make_async_copy(keys_ref, out_ref.at[:slots], sems.at[0]),
        pltpu.make_async_copy(values_ref, out_ref.at[slots:], sems.at[1]),
    ]
    for copy in copies:
        copy.start()
    for copy in copies:
        copy.wait()


def fetch_kernel(map_ref, ids_ref, stream_ref, saved_ref, grad_ref, *refs):
    saved_near, grad_near, sent_ref, place_ref, map_near, ids_near, sems = refs
    rows = sent_ref.at[: stream_ref.shape[0]]
    section = lax.axis_index("pipe")
    small = [
        pltpu.make_async_copy(map_ref, map_near, sems.at[0]),
        pltpu.make_async_copy(ids_ref, ids_near, sems.at[1]),
    ]
    large = [
        pltpu.make_async_copy(saved_ref, saved_near, sems.at[2]),
        pltpu.make_async_copy(grad_ref, grad_near, sems.at[3]),
    ]
    for copy in small + large:
        copy.start()

    @pl.when(section == 0)
    def _():
        pltpu.make_async_copy(stream_ref, rows, sems.at[4]).start()

    @pl.when(section != 0)
    def _():
        pltpu.make_async_copy(grad_ref, rows, sems.at[4]).start()

    for copy in small:
        copy.wait()
    for i in range(place_ref.shape[0]):
        place_ref[i] = map_near[ids_near[i]]
    for copy in large:
        copy.wait()
    pltpu.make_async_copy(grad_ref, rows, sems.at[4]).wait()


def score_kernel(slots, place_ref, saved_ref, grad_ref, rows_ref, *refs):
    memory, (terms_ref, sent_ref) = refs[:-2], refs[-2:]
    me = lax.axis_index("dp")
    tokens, width = saved_ref.shape
    heads = width // HEAD_DIM
    back = place_ref[1]
    owner, slot = back // slots, back % slots
    keys = pick(memory, 0, owner, slot, me)
    values = pick(memory, slots, owner, slot, me)
    count = keys.shape[0]
    saved, grads = saved_ref[...], grad_ref[...]
    weights = softmax_t(by_head(keys), saved, heads)
    grad_weights = dot(by_head(values), grads, NT).reshape(weights.shape)
    centre = jnp.sum(weights * grad_weights, axis=1, keepdims=True)
    grad_scores = weights * (grad_weights - centre) * (1.0 / math.sqrt(HEAD_DIM))
    flat = heads * count
    grad_scores = grad_scores.astype(jnp.bfloat16).reshape(flat, tokens)
    rounded = weights.astype(jnp.bfloat16).reshape(flat, tokens)
    terms_ref[:, :width] = own_head(dot(grad_scores, saved, NN), count).astype(jnp.bfloat16)
    terms_ref[:, width : 2 * width] = own_head(dot(rounded, grads, NN), count).astype(jnp.bfloat16)
    place = jnp.full((count, HEAD_DIM), back, jnp.int32)
    terms_ref[:, 2 * width :] = place.astype(jnp.float32).astype(jnp.bfloat16)
    first, second = tokens, tokens + padded(count)
    section = lax.axis_index("pipe")

    @pl.when(section == 0)
    def _():
        ahead = place_ref[0]
        owner, slot = ahead // slots, ahead % slots
        sent_ref[first : first + count, :] = pick(memory, 0, owner, slot, me)
        sent_ref[second : second + count, :] = pick(memory, slots, owner, slot, me)

    @pl.when(section != 0)
    def _():
        sent_ref[first : first + count, :] = keys
        part = flat * tokens // width
        for i in range(width // tokens):
            at = slice(i * tokens, (i + 1) * tokens)
            sent_ref[second : second + part, at] = grad_scores[i * part : (i + 1) * part, :]


def output_kernel(tokens, count, sent_ref, next_ref, back_ref):
    width = sent_ref.shape[1]
    heads = width // HEAD_DIM
    first, second = tokens, tokens + padded(count)
    keys = by_head(sent_ref[first : first + count, :])
    rows = sent_ref[:tokens, :]
    section = lax.axis_index("pipe")

    @pl.when(section == 0)
    def _():
        next_ref[...] = jnp.zeros_like(next_ref)
        part = heads * count * tokens // width
        grad_scores = [
            sent_ref[second : second + part, i * tokens : (i + 1) * tokens]
            for i in range(width // tokens)
        ]
        added = dot(jnp.concatenate(grad_scores, axis=0), keys, TN)
        back_ref[...] = (rows.astype(jnp.float32) + added).astype(jnp.bfloat16)

    @pl.when(section != 0)
    def _():
        back_ref[...] = jnp.zeros_like(back_ref)
        values = by_head(sent_ref[second : second + count, :])
        weights = softmax_t(keys, rows, heads).astype(jnp.bfloat16).reshape(-1, tokens)
        added = dot(weights, values, TN)
        next_ref[...] = (rows.astype(jnp.float32) + added).astype(jnp.bfloat16)


def sum_kernel(slots, *refs):
    terms_refs, (key_ref, value_ref) = refs[:-2], refs[-2:]
    me = lax.axis_index("dp")
    width = key_ref.shape[2]
    tiles = width // HEAD_DIM
    terms = [ref[...].astype(jnp.float32) for ref in terms_refs]
    for slot in range(slots):
        here = (me * slots + slot).astype(jnp.float32)
        hits = [t[:, 2 * width :] == here for t in terms]
        for i in range(2 * tiles):
            at = slice(i * HEAD_DIM, (i + 1) * HEAD_DIM)
            total = sum(jnp.where(hit, t[:, at], 0.0) for hit, t in zip(hits, terms))
            out, j = (key_ref, i) if i < tiles else (value_ref, i - tiles)
            out[slot, :, j * HEAD_DIM : (j + 1) * HEAD_DIM] = total.astype(jnp.bfloat16)


def around(x, replicas, order):
    parts = {0: x}
    for d in order:
        parts[d] = lax.ppermute(x, "dp", [(i, i ^ d) for i in range(replicas)])
    return [parts[d] for d in range(replicas)]


def vmem(x):
    return pltpu.with_memory_space_constraint(x, pltpu.VMEM)


def hbm(x):
    return pltpu.with_memory_space_constraint(x, pltpu.HBM)


def smem(x):
    return pltpu.with_memory_space_constraint(x, pltpu.SMEM)


def call(kernel, name, out, in_specs, scratch=(), moved=0, aliases=()):
    return pl.pallas_call(
        kernel,
        out_shape=out,
        in_specs=in_specs,
        out_specs=jax.tree.map(lambda o: SMEM if o.shape == (2,) else VMEM, out),
        scratch_shapes=scratch,
        input_output_aliases=dict(aliases),
        compiler_params=pltpu.CompilerParams(vmem_limit_bytes=16 * 1024 * 1024),
        cost_estimate=pl.CostEstimate(flops=0, bytes_accessed=moved, transcendentals=0),
        name=name,
    )


def direct(stream_in, saved_in, grad_out, mem_keys, mem_values, owner_map, block_ids):
    replicas = lax.axis_size("dp")
    slots, block_rows, width = mem_keys.shape[1:]
    tokens = stream_in.shape[1]
    rows = pltpu.VMEM((tokens, width), jnp.bfloat16)
    grad_lines = width // HEAD_DIM * block_rows * tokens // width
    sent_rows = tokens + padded(block_rows) + padded(max(block_rows, grad_lines))
    sent = pltpu.VMEM((sent_rows, width), jnp.bfloat16)
    stacked = call(
        stack_kernel,
        "stack",
        pltpu.VMEM((2 * slots, block_rows, width), jnp.bfloat16),
        [HBM] * 2,
        [pltpu.SemaphoreType.DMA((2,))],
    )(hbm(mem_keys[0]), hbm(mem_values[0]))
    stacked, *own = lax.optimization_barrier(
        (stacked, owner_map, block_ids.reshape(-1), stream_in[0], saved_in[0], grad_out[0])
    )
    memory = around(stacked, replicas, FETCH_ORDER)
    saved, grads, to_send, places = call(
        fetch_kernel,
        "fetch",
        (rows, rows, sent, pltpu.SMEM((2,), jnp.int32)),
        [HBM] * 5,
        [
            pltpu.SMEM(owner_map.shape, jnp.int32),
            pltpu.SMEM((2,), jnp.int32),
            pltpu.SemaphoreType.DMA((5,)),
        ],
        12 * tokens * width,
    )(*map(hbm, own))
    terms, to_send = call(
        functools.partial(score_kernel, slots),
        "scores",
        (pltpu.VMEM((block_rows, 2 * width + HEAD_DIM), jnp.bfloat16), sent),
        [SMEM] + [VMEM] * (3 + replicas),
        aliases={3: 1}.items(),
    )(smem(places), *map(vmem, (saved, grads, to_send, *memory)))
    other_sent = lax.ppermute(to_send, "pipe", [(0, 1), (1, 0)])
    term_parts = around(terms, replicas, SEND_ORDER)
    next_input, grad_back = call(
        functools.partial(output_kernel, tokens, block_rows),
        "outputs",
        (jax.ShapeDtypeStruct((tokens, width), jnp.bfloat16),) * 2,
        [VMEM],
        (),
        4 * tokens * width,
    )(vmem(other_sent))
    *term_parts, next_input, grad_back = lax.optimization_barrier((*term_parts, next_input, grad_back))
    key_grad, value_grad = call(
        functools.partial(sum_kernel, slots),
        "sums",
        (jax.ShapeDtypeStruct((slots, block_rows, width), jnp.bfloat16),) * 2,
        [VMEM] * replicas,
    )(*map(vmem, term_parts))
    return next_input[None], grad_back[None], key_grad[None], value_grad[None]


def from_behind(x, axis, by):
    peers = lax.axis_size(axis)
    pairs = [(i, i + by) for i in range(peers) if 0 <= i + by < peers]
    return lax.ppermute(x, axis, pairs)


def forward_part(inputs, memory_keys, memory_values):
    rows = inputs.shape[0]
    heads_count = inputs.shape[1] // HEAD_DIM
    scale = 1.0 / math.sqrt(HEAD_DIM)
    queries = inputs.reshape(rows, heads_count, HEAD_DIM)
    key_rows = memory_keys.reshape(-1, heads_count, HEAD_DIM)
    value_rows = memory_values.reshape(-1, heads_count, HEAD_DIM)
    scores = (
        jnp.einsum("thd,khd->htk", queries, key_rows, preferred_element_type=jnp.float32) * scale
    )
    exponent = jnp.exp(scores - jnp.max(scores, axis=-1, keepdims=True))
    weights = exponent / jnp.sum(exponent, axis=-1, keepdims=True)
    rounded = weights.astype(jnp.bfloat16)
    attended = jnp.einsum(
        "htk,khd->thd", rounded, value_rows, preferred_element_type=jnp.float32
    ).reshape(rows, -1)
    return (queries, key_rows, value_rows, weights, rounded, attended)


def backward_part(inputs, grads, memory_keys, memory_values):
    queries, key_rows, value_rows, weights, rounded, attended = forward_part(
        inputs, memory_keys, memory_values
    )
    rows = inputs.shape[0]
    heads_count = queries.shape[1]
    scale = 1.0 / math.sqrt(HEAD_DIM)
    grad_rows = grads.reshape(rows, heads_count, HEAD_DIM)
    grad_weights = jnp.einsum(
        "thd,khd->htk", grad_rows, value_rows, preferred_element_type=jnp.float32
    )
    centre = jnp.sum(weights * grad_weights, axis=-1, keepdims=True)
    grad_scores = (weights * (grad_weights - centre) * scale).astype(jnp.bfloat16)
    grad_queries = jnp.einsum(
        "htk,khd->thd", grad_scores, key_rows, preferred_element_type=jnp.float32
    ).reshape(rows, -1)
    key_terms = jnp.einsum("htk,thd->khd", grad_scores, queries, preferred_element_type=jnp.float32)
    value_terms = jnp.einsum("htk,thd->khd", rounded, grad_rows, preferred_element_type=jnp.float32)
    input_grad = (grads.astype(jnp.float32) + grad_queries).astype(jnp.bfloat16)
    key_count = key_rows.shape[0]
    return (
        input_grad,
        key_terms.reshape(key_count, -1).astype(jnp.bfloat16),
        value_terms.reshape(key_count, -1).astype(jnp.bfloat16),
    )


def routed(stream_in, saved_in, grad_out, mem_keys, mem_values, owner_map, block_ids):
    replicas = lax.axis_size("dp")
    local_blocks = mem_keys.shape[1]
    block_rows = mem_keys.shape[2]
    width = stream_in.shape[2]
    table_size = owner_map.shape[0]
    requested = block_ids.reshape(-1)
    picks = requested.shape[0]
    half = picks // 2
    matches = requested[:, None] == jnp.arange(table_size, dtype=jnp.int32)[None, :]
    places = jnp.sum(jnp.where(matches, owner_map[None, :], 0), axis=1)
    owners = places // local_blocks
    slot_ids = places % local_blocks
    owner_hits = owners[:, None] == jnp.arange(replicas, dtype=jnp.int32)[None, :]
    served = None
    wanted = jnp.sum(jnp.where(owner_hits, slot_ids[:, None], 0), axis=0)
    served = lax.all_to_all(
        wanted.reshape(replicas, 1), "dp", split_axis=0, concat_axis=0, tiled=True
    ).reshape(replicas)
    out_keys = jnp.take(mem_keys[0], served, axis=0)
    out_values = jnp.take(mem_values[0], served, axis=0)
    got_keys, got_values = (
        lax.all_to_all(out_keys, "dp", split_axis=0, concat_axis=0, tiled=True),
        lax.all_to_all(out_values, "dp", split_axis=0, concat_axis=0, tiled=True),
    )
    fetched_keys = jnp.take(got_keys, owners, axis=0)
    fetched_values = jnp.take(got_values, owners, axis=0)
    forward_keys = fetched_keys[:half].reshape(-1, width)
    forward_values = fetched_values[:half].reshape(-1, width)
    backward_keys = fetched_keys[half:].reshape(-1, width)
    backward_values = fetched_values[half:].reshape(-1, width)
    attended = forward_part(stream_in[0], forward_keys, forward_values)[5]
    section_out = (stream_in[0].astype(jnp.float32) + attended).astype(jnp.bfloat16)
    next_input = from_behind(section_out[None], "pipe", 1)
    input_grad, key_terms, value_terms = backward_part(
        saved_in[0], grad_out[0], backward_keys, backward_values
    )
    grad_back = from_behind(input_grad[None], "pipe", -1)
    key_blocks = key_terms.reshape(half, block_rows, width)
    value_blocks = value_terms.reshape(half, block_rows, width)
    back_hits = owner_hits[half:].astype(jnp.bfloat16)
    send_keys = jnp.einsum(
        "ro,rtf->otf", back_hits, key_blocks, preferred_element_type=jnp.float32
    ).astype(jnp.bfloat16)
    send_values = jnp.einsum(
        "ro,rtf->otf", back_hits, value_blocks, preferred_element_type=jnp.float32
    ).astype(jnp.bfloat16)
    recv_keys, recv_values = (
        lax.all_to_all(send_keys, "dp", split_axis=0, concat_axis=0, tiled=True),
        lax.all_to_all(send_values, "dp", split_axis=0, concat_axis=0, tiled=True),
    )
    slot_hits = (served[:, None] == jnp.arange(local_blocks, dtype=jnp.int32)[None, :]).astype(
        jnp.bfloat16
    )
    key_grad = jnp.einsum(
        "sm,stf->mtf", slot_hits, recv_keys, preferred_element_type=jnp.float32
    ).astype(jnp.bfloat16)
    value_grad = jnp.einsum(
        "sm,stf->mtf", slot_hits, recv_values, preferred_element_type=jnp.float32
    ).astype(jnp.bfloat16)
    return (next_input, grad_back, key_grad[None], value_grad[None])


def local(*args):
    replicas, (_, tokens, width) = lax.axis_size("dp"), args[0].shape
    few = replicas <= DIRECT_REPLICAS and replicas & (replicas - 1) == 0
    one_each = args[-1].size == 2 and lax.axis_size("pipe") == 2 and width % tokens == 0
    return (direct if few and one_each else routed)(*args)


def solution(mesh):
    in_specs = (
        P("pipe", "dp", "tensor"),
        P("pipe", "dp", "tensor"),
        P("pipe", "dp", "tensor"),
        P("pipe", "dp", None, "tensor"),
        P("pipe", "dp", None, "tensor"),
        P(),
        P(None, "pipe", "dp", None),
    )
    out_specs = (
        P("pipe", "dp", "tensor"),
        P("pipe", "dp", "tensor"),
        P("pipe", "dp", None, "tensor"),
        P("pipe", "dp", None, "tensor"),
    )
    return jax.shard_map(local, mesh=mesh, in_specs=in_specs, out_specs=out_specs, check_vma=False)
```

```python
import functools
import math

import jax
import jax.numpy as jnp
from jax import lax
from jax.experimental import pallas as pl
from jax.experimental.pallas import tpu as pltpu
from jax.sharding import PartitionSpec as P

HEAD_DIM = 128
DIRECT_REPLICAS = 8
HBM = pl.BlockSpec(memory_space=pltpu.HBM)
VMEM = pl.BlockSpec(memory_space=pltpu.VMEM)
SMEM = pl.BlockSpec(memory_space=pltpu.SMEM)
NT = (((1,), (1,)), ((), ()))
NN = (((1,), (0,)), ((), ()))
TN = (((0,), (0,)), ((), ()))


def padded(rows):
    return -(-rows // 16) * 16


def dot(a, b, dims):
    return lax.dot_general(a, b, dims, preferred_element_type=jnp.float32)


def by_head(block):
    keys, width = block.shape
    heads = width // HEAD_DIM
    wide = jnp.broadcast_to(block.astype(jnp.float32)[None], (heads, keys, width))
    head = lax.broadcasted_iota(jnp.int32, wide.shape, 0)
    feature_head = lax.broadcasted_iota(jnp.int32, wide.shape, 2) // HEAD_DIM
    return jnp.where(head == feature_head, wide, 0.0).reshape(heads * keys, width).astype(block.dtype)


def own_head(product, keys):
    heads = product.shape[0] // keys
    parts = [
        product[h * keys : (h + 1) * keys, h * HEAD_DIM : (h + 1) * HEAD_DIM] for h in range(heads)
    ]
    return jnp.concatenate(parts, axis=1)


def softmax_t(keys_by_head, rows, heads):
    scores = dot(keys_by_head, rows, NT) * (1.0 / math.sqrt(HEAD_DIM))
    scores = scores.reshape(heads, -1, rows.shape[0])
    exponent = jnp.exp(scores - jnp.max(scores, axis=1, keepdims=True))
    return exponent / jnp.sum(exponent, axis=1, keepdims=True)


def pick(refs, first, behind, slot):
    block = refs[0][first + slot]
    for i in range(1, len(refs)):
        block = jnp.where(behind == len(refs) - i, refs[i][first + slot], block)
    return block


def stack_kernel(keys_ref, values_ref, out_ref, sems):
    slots = keys_ref.shape[0]
    copies = [
        pltpu.make_async_copy(keys_ref, out_ref.at[:slots], sems.at[0]),
        pltpu.make_async_copy(values_ref, out_ref.at[slots:], sems.at[1]),
    ]
    for copy in copies:
        copy.start()
    for copy in copies:
        copy.wait()


def fetch_kernel(map_ref, ids_ref, stream_ref, saved_ref, grad_ref, *refs):
    saved_near, grad_near, sent_ref, place_ref, map_near, ids_near, sems = refs
    rows = sent_ref.at[: stream_ref.shape[0]]
    section = lax.axis_index("pipe")
    small = [
        pltpu.make_async_copy(map_ref, map_near, sems.at[0]),
        pltpu.make_async_copy(ids_ref, ids_near, sems.at[1]),
    ]
    large = [
        pltpu.make_async_copy(saved_ref, saved_near, sems.at[2]),
        pltpu.make_async_copy(grad_ref, grad_near, sems.at[3]),
    ]
    for copy in small + large:
        copy.start()

    @pl.when(section == 0)
    def _():
        pltpu.make_async_copy(stream_ref, rows, sems.at[4]).start()

    @pl.when(section != 0)
    def _():
        pltpu.make_async_copy(grad_ref, rows, sems.at[4]).start()

    for copy in small:
        copy.wait()
    for i in range(place_ref.shape[0]):
        place_ref[i] = map_near[ids_near[i]]
    for copy in large:
        copy.wait()
    pltpu.make_async_copy(grad_ref, rows, sems.at[4]).wait()


def score_kernel(slots, place_ref, saved_ref, grad_ref, rows_ref, *refs):
    memory, (terms_ref, sent_ref) = refs[:-2], refs[-2:]
    me = lax.axis_index("dp")
    section = lax.axis_index("pipe")
    tokens, width = saved_ref.shape
    heads = width // HEAD_DIM
    back = place_ref[1]
    behind, slot = lax.rem(me - back // slots + len(memory), len(memory)), back % slots
    keys = pick(memory, 0, behind, slot)
    values = pick(memory, slots, behind, slot)
    count = keys.shape[0]
    saved, grads = saved_ref[...], grad_ref[...]
    weights = softmax_t(by_head(keys), saved, heads)
    grad_weights = dot(by_head(values), grads, NT).reshape(weights.shape)
    centre = jnp.sum(weights * grad_weights, axis=1, keepdims=True)
    grad_scores = weights * (grad_weights - centre) * (1.0 / math.sqrt(HEAD_DIM))
    flat = heads * count
    grad_scores = grad_scores.astype(jnp.bfloat16).reshape(flat, tokens)
    rounded = weights.astype(jnp.bfloat16).reshape(flat, tokens)
    terms_ref[:, :width] = own_head(dot(grad_scores, saved, NN), count).astype(jnp.bfloat16)
    terms_ref[:, width : 2 * width] = own_head(dot(rounded, grads, NN), count).astype(jnp.bfloat16)
    place = jnp.full((count, HEAD_DIM), back, jnp.int32)
    terms_ref[:, 2 * width :] = place.astype(jnp.float32).astype(jnp.bfloat16)
    first, second = tokens, tokens + padded(count)

    @pl.when(section == 0)
    def _():
        ahead = place_ref[0]
        behind, slot = lax.rem(me - ahead // slots + len(memory), len(memory)), ahead % slots
        sent_ref[first : first + count, :] = pick(memory, 0, behind, slot)
        sent_ref[second : second + count, :] = pick(memory, slots, behind, slot)

    @pl.when(section != 0)
    def _():
        sent_ref[first : first + count, :] = keys
        part = flat * tokens // width
        for i in range(width // tokens):
            at = slice(i * tokens, (i + 1) * tokens)
            sent_ref[second : second + part, at] = grad_scores[i * part : (i + 1) * part, :]


def output_kernel(tokens, count, sent_ref, next_ref, back_ref):
    width = sent_ref.shape[1]
    heads = width // HEAD_DIM
    first, second = tokens, tokens + padded(count)
    keys = by_head(sent_ref[first : first + count, :])
    rows = sent_ref[:tokens, :]
    section = lax.axis_index("pipe")

    @pl.when(section == 0)
    def _():
        next_ref[...] = jnp.zeros_like(next_ref)
        part = heads * count * tokens // width
        grad_scores = [
            sent_ref[second : second + part, i * tokens : (i + 1) * tokens]
            for i in range(width // tokens)
        ]
        added = dot(jnp.concatenate(grad_scores, axis=0), keys, TN)
        back_ref[...] = (rows.astype(jnp.float32) + added).astype(jnp.bfloat16)

    @pl.when(section != 0)
    def _():
        back_ref[...] = jnp.zeros_like(back_ref)
        values = by_head(sent_ref[second : second + count, :])
        weights = softmax_t(keys, rows, heads).astype(jnp.bfloat16).reshape(-1, tokens)
        added = dot(weights, values, TN)
        next_ref[...] = (rows.astype(jnp.float32) + added).astype(jnp.bfloat16)


def sum_kernel(slots, *refs):
    terms_refs, (key_ref, value_ref) = refs[:-2], refs[-2:]
    me = lax.axis_index("dp")
    width = key_ref.shape[2]
    tiles = width // HEAD_DIM
    terms = [ref[...].astype(jnp.float32) for ref in terms_refs]
    for slot in range(slots):
        here = (me * slots + slot).astype(jnp.float32)
        hits = [t[:, 2 * width :] == here for t in terms]
        for i in range(2 * tiles):
            at = slice(i * HEAD_DIM, (i + 1) * HEAD_DIM)
            total = sum(jnp.where(hit, t[:, at], 0.0) for hit, t in zip(hits, terms))
            out, j = (key_ref, i) if i < tiles else (value_ref, i - tiles)
            out[slot, :, j * HEAD_DIM : (j + 1) * HEAD_DIM] = total.astype(jnp.bfloat16)


def exchange(x, replicas):
    return [x] + [
        lax.ppermute(x, "dp", [(i, (i + d) % replicas) for i in range(replicas)])
        for d in range(replicas - 1, 0, -1)
    ]


def vmem(x):
    return pltpu.with_memory_space_constraint(x, pltpu.VMEM)


def hbm(x):
    return pltpu.with_memory_space_constraint(x, pltpu.HBM)


def smem(x):
    return pltpu.with_memory_space_constraint(x, pltpu.SMEM)


def call(kernel, name, out, in_specs, scratch=(), moved=0, aliases=()):
    return pl.pallas_call(
        kernel,
        out_shape=out,
        in_specs=in_specs,
        out_specs=jax.tree.map(lambda o: SMEM if o.shape == (2,) else VMEM, out),
        scratch_shapes=scratch,
        input_output_aliases=dict(aliases),
        compiler_params=pltpu.CompilerParams(vmem_limit_bytes=16 * 1024 * 1024),
        cost_estimate=pl.CostEstimate(flops=0, bytes_accessed=moved, transcendentals=0),
        name=name,
    )


def direct(stream_in, saved_in, grad_out, mem_keys, mem_values, owner_map, block_ids):
    replicas = lax.axis_size("dp")
    slots, block_rows, width = mem_keys.shape[1:]
    tokens = stream_in.shape[1]
    rows = pltpu.VMEM((tokens, width), jnp.bfloat16)
    grad_lines = width // HEAD_DIM * block_rows * tokens // width
    sent_rows = tokens + padded(block_rows) + padded(max(block_rows, grad_lines))
    sent = pltpu.VMEM((sent_rows, width), jnp.bfloat16)
    stacked = call(
        stack_kernel,
        "stack",
        pltpu.VMEM((2 * slots, block_rows, width), jnp.bfloat16),
        [HBM] * 2,
        [pltpu.SemaphoreType.DMA((2,))],
    )(hbm(mem_keys[0]), hbm(mem_values[0]))
    stacked, *own = lax.optimization_barrier(
        (stacked, owner_map, block_ids.reshape(-1), stream_in[0], saved_in[0], grad_out[0])
    )
    memory = exchange(stacked, replicas)
    saved, grads, to_send, places = call(
        fetch_kernel,
        "fetch",
        (rows, rows, sent, pltpu.SMEM((2,), jnp.int32)),
        [HBM] * 5,
        [
            pltpu.SMEM(owner_map.shape, jnp.int32),
            pltpu.SMEM((2,), jnp.int32),
            pltpu.SemaphoreType.DMA((5,)),
        ],
        12 * tokens * width,
    )(*map(hbm, own))
    terms, to_send = call(
        functools.partial(score_kernel, slots),
        "scores",
        (pltpu.VMEM((block_rows, 2 * width + HEAD_DIM), jnp.bfloat16), sent),
        [SMEM] + [VMEM] * (3 + replicas),
        aliases={3: 1}.items(),
    )(smem(places), *map(vmem, (saved, grads, to_send, *memory)))
    other_sent = lax.ppermute(to_send, "pipe", [(0, 1), (1, 0)])
    term_parts = exchange(terms, replicas)
    next_input, grad_back = call(
        functools.partial(output_kernel, tokens, block_rows),
        "outputs",
        (jax.ShapeDtypeStruct((tokens, width), jnp.bfloat16),) * 2,
        [VMEM],
        (),
        4 * tokens * width,
    )(vmem(other_sent))
    *term_parts, next_input, grad_back = lax.optimization_barrier((*term_parts, next_input, grad_back))
    key_grad, value_grad = call(
        functools.partial(sum_kernel, slots),
        "sums",
        (jax.ShapeDtypeStruct((slots, block_rows, width), jnp.bfloat16),) * 2,
        [VMEM] * replicas,
    )(*map(vmem, term_parts))
    return next_input[None], grad_back[None], key_grad[None], value_grad[None]


def from_behind(x, axis, by):
    peers = lax.axis_size(axis)
    pairs = [(i, i + by) for i in range(peers) if 0 <= i + by < peers]
    return lax.ppermute(x, axis, pairs)


def forward_part(inputs, memory_keys, memory_values):
    rows = inputs.shape[0]
    heads_count = inputs.shape[1] // HEAD_DIM
    scale = 1.0 / math.sqrt(HEAD_DIM)
    queries = inputs.reshape(rows, heads_count, HEAD_DIM)
    key_rows = memory_keys.reshape(-1, heads_count, HEAD_DIM)
    value_rows = memory_values.reshape(-1, heads_count, HEAD_DIM)
    scores = (
        jnp.einsum("thd,khd->htk", queries, key_rows, preferred_element_type=jnp.float32) * scale
    )
    exponent = jnp.exp(scores - jnp.max(scores, axis=-1, keepdims=True))
    weights = exponent / jnp.sum(exponent, axis=-1, keepdims=True)
    rounded = weights.astype(jnp.bfloat16)
    attended = jnp.einsum(
        "htk,khd->thd", rounded, value_rows, preferred_element_type=jnp.float32
    ).reshape(rows, -1)
    return (queries, key_rows, value_rows, weights, rounded, attended)


def backward_part(inputs, grads, memory_keys, memory_values):
    queries, key_rows, value_rows, weights, rounded, attended = forward_part(
        inputs, memory_keys, memory_values
    )
    rows = inputs.shape[0]
    heads_count = queries.shape[1]
    scale = 1.0 / math.sqrt(HEAD_DIM)
    grad_rows = grads.reshape(rows, heads_count, HEAD_DIM)
    grad_weights = jnp.einsum(
        "thd,khd->htk", grad_rows, value_rows, preferred_element_type=jnp.float32
    )
    centre = jnp.sum(weights * grad_weights, axis=-1, keepdims=True)
    grad_scores = (weights * (grad_weights - centre) * scale).astype(jnp.bfloat16)
    grad_queries = jnp.einsum(
        "htk,khd->thd", grad_scores, key_rows, preferred_element_type=jnp.float32
    ).reshape(rows, -1)
    key_terms = jnp.einsum("htk,thd->khd", grad_scores, queries, preferred_element_type=jnp.float32)
    value_terms = jnp.einsum("htk,thd->khd", rounded, grad_rows, preferred_element_type=jnp.float32)
    input_grad = (grads.astype(jnp.float32) + grad_queries).astype(jnp.bfloat16)
    key_count = key_rows.shape[0]
    return (
        input_grad,
        key_terms.reshape(key_count, -1).astype(jnp.bfloat16),
        value_terms.reshape(key_count, -1).astype(jnp.bfloat16),
    )


def routed(stream_in, saved_in, grad_out, mem_keys, mem_values, owner_map, block_ids):
    replicas = lax.axis_size("dp")
    local_blocks = mem_keys.shape[1]
    block_rows = mem_keys.shape[2]
    width = stream_in.shape[2]
    table_size = owner_map.shape[0]
    requested = block_ids.reshape(-1)
    picks = requested.shape[0]
    half = picks // 2
    matches = requested[:, None] == jnp.arange(table_size, dtype=jnp.int32)[None, :]
    places = jnp.sum(jnp.where(matches, owner_map[None, :], 0), axis=1)
    owners = places // local_blocks
    slot_ids = places % local_blocks
    owner_hits = owners[:, None] == jnp.arange(replicas, dtype=jnp.int32)[None, :]
    served = None
    wanted = jnp.sum(jnp.where(owner_hits, slot_ids[:, None], 0), axis=0)
    served = lax.all_to_all(
        wanted.reshape(replicas, 1), "dp", split_axis=0, concat_axis=0, tiled=True
    ).reshape(replicas)
    out_keys = jnp.take(mem_keys[0], served, axis=0)
    out_values = jnp.take(mem_values[0], served, axis=0)
    got_keys, got_values = (
        lax.all_to_all(out_keys, "dp", split_axis=0, concat_axis=0, tiled=True),
        lax.all_to_all(out_values, "dp", split_axis=0, concat_axis=0, tiled=True),
    )
    fetched_keys = jnp.take(got_keys, owners, axis=0)
    fetched_values = jnp.take(got_values, owners, axis=0)
    forward_keys = fetched_keys[:half].reshape(-1, width)
    forward_values = fetched_values[:half].reshape(-1, width)
    backward_keys = fetched_keys[half:].reshape(-1, width)
    backward_values = fetched_values[half:].reshape(-1, width)
    attended = forward_part(stream_in[0], forward_keys, forward_values)[5]
    section_out = (stream_in[0].astype(jnp.float32) + attended).astype(jnp.bfloat16)
    next_input = from_behind(section_out[None], "pipe", 1)
    input_grad, key_terms, value_terms = backward_part(
        saved_in[0], grad_out[0], backward_keys, backward_values
    )
    grad_back = from_behind(input_grad[None], "pipe", -1)
    key_blocks = key_terms.reshape(half, block_rows, width)
    value_blocks = value_terms.reshape(half, block_rows, width)
    back_hits = owner_hits[half:].astype(jnp.bfloat16)
    send_keys = jnp.einsum(
        "ro,rtf->otf", back_hits, key_blocks, preferred_element_type=jnp.float32
    ).astype(jnp.bfloat16)
    send_values = jnp.einsum(
        "ro,rtf->otf", back_hits, value_blocks, preferred_element_type=jnp.float32
    ).astype(jnp.bfloat16)
    recv_keys, recv_values = (
        lax.all_to_all(send_keys, "dp", split_axis=0, concat_axis=0, tiled=True),
        lax.all_to_all(send_values, "dp", split_axis=0, concat_axis=0, tiled=True),
    )
    slot_hits = (served[:, None] == jnp.arange(local_blocks, dtype=jnp.int32)[None, :]).astype(
        jnp.bfloat16
    )
    key_grad = jnp.einsum(
        "sm,stf->mtf", slot_hits, recv_keys, preferred_element_type=jnp.float32
    ).astype(jnp.bfloat16)
    value_grad = jnp.einsum(
        "sm,stf->mtf", slot_hits, recv_values, preferred_element_type=jnp.float32
    ).astype(jnp.bfloat16)
    return (next_input, grad_back, key_grad[None], value_grad[None])


def local(*args):
    replicas, (_, tokens, width) = lax.axis_size("dp"), args[0].shape
    few = replicas <= DIRECT_REPLICAS
    one_each = args[-1].size == 2 and lax.axis_size("pipe") == 2 and width % tokens == 0
    return (direct if few and one_each else routed)(*args)


def solution(mesh):
    in_specs = (
        P("pipe", "dp", "tensor"),
        P("pipe", "dp", "tensor"),
        P("pipe", "dp", "tensor"),
        P("pipe", "dp", None, "tensor"),
        P("pipe", "dp", None, "tensor"),
        P(),
        P(None, "pipe", "dp", None),
    )
    out_specs = (
        P("pipe", "dp", "tensor"),
        P("pipe", "dp", "tensor"),
        P("pipe", "dp", None, "tensor"),
        P("pipe", "dp", None, "tensor"),
    )
    return jax.shard_map(local, mesh=mesh, in_specs=in_specs, out_specs=out_specs, check_vma=False)
```

```python
import functools
import math

import jax
import jax.numpy as jnp
from jax import lax
from jax.experimental import pallas as pl
from jax.experimental.pallas import tpu as pltpu
from jax.sharding import PartitionSpec as P

HEAD_DIM = 128
DIRECT_REPLICAS = 8
HBM = pl.BlockSpec(memory_space=pltpu.HBM)
VMEM = pl.BlockSpec(memory_space=pltpu.VMEM)
SMEM = pl.BlockSpec(memory_space=pltpu.SMEM)
NT = (((1,), (1,)), ((), ()))
NN = (((1,), (0,)), ((), ()))
TN = (((0,), (0,)), ((), ()))


def padded(rows):
    return -(-rows // 16) * 16


def dot(a, b, dims):
    return lax.dot_general(a, b, dims, preferred_element_type=jnp.float32)


def by_head(block):
    keys, width = block.shape
    heads = width // HEAD_DIM
    wide = jnp.broadcast_to(block.astype(jnp.float32)[None], (heads, keys, width))
    head = lax.broadcasted_iota(jnp.int32, wide.shape, 0)
    feature_head = lax.broadcasted_iota(jnp.int32, wide.shape, 2) // HEAD_DIM
    return jnp.where(head == feature_head, wide, 0.0).reshape(heads * keys, width).astype(block.dtype)


def groups(width):
    step = min(width, 2 * HEAD_DIM)
    return [slice(i, i + step) for i in range(0, width, step)]


def per_head(block, rows):
    parts = [dot(by_head(block[:, at]), rows[:, at], NT) for at in groups(rows.shape[1])]
    return jnp.concatenate(parts, axis=0).reshape(-1, block.shape[0], rows.shape[0])


def reduced(by_key, rows):
    keys, tokens = by_key.shape[1:]
    parts = []
    for at in groups(rows.shape[1]):
        heads = slice(at.start // HEAD_DIM, at.stop // HEAD_DIM)
        product = dot(by_key[heads].reshape(-1, tokens), rows[:, at], NN)
        parts += [
            product[h * keys : (h + 1) * keys, h * HEAD_DIM : (h + 1) * HEAD_DIM]
            for h in range(heads.stop - heads.start)
        ]
    return jnp.concatenate(parts, axis=1)


def softmax_t(keys, rows):
    scores = per_head(keys, rows) * (1.0 / math.sqrt(HEAD_DIM))
    exponent = jnp.exp(scores - jnp.max(scores, axis=1, keepdims=True))
    return exponent / jnp.sum(exponent, axis=1, keepdims=True)


def pick(refs, first, behind, slot):
    block = refs[0][first + slot]
    for i in range(1, len(refs)):
        block = jnp.where(behind == len(refs) - i, refs[i][first + slot], block)
    return block


def stack_kernel(keys_ref, values_ref, out_ref, sems):
    slots = keys_ref.shape[0]
    copies = [
        pltpu.make_async_copy(keys_ref, out_ref.at[:slots], sems.at[0]),
        pltpu.make_async_copy(values_ref, out_ref.at[slots:], sems.at[1]),
    ]
    for copy in copies:
        copy.start()
    for copy in copies:
        copy.wait()


def fetch_kernel(map_ref, ids_ref, stream_ref, saved_ref, grad_ref, *refs):
    saved_near, grad_near, sent_ref, place_ref, map_near, ids_near, sems = refs
    rows = sent_ref.at[: stream_ref.shape[0]]
    section = lax.axis_index("pipe")
    small = [
        pltpu.make_async_copy(map_ref, map_near, sems.at[0]),
        pltpu.make_async_copy(ids_ref, ids_near, sems.at[1]),
    ]
    large = [
        pltpu.make_async_copy(saved_ref, saved_near, sems.at[2]),
        pltpu.make_async_copy(grad_ref, grad_near, sems.at[3]),
    ]
    for copy in small + large:
        copy.start()

    @pl.when(section == 0)
    def _():
        pltpu.make_async_copy(stream_ref, rows, sems.at[4]).start()

    @pl.when(section != 0)
    def _():
        pltpu.make_async_copy(grad_ref, rows, sems.at[4]).start()

    for copy in small:
        copy.wait()
    for i in range(place_ref.shape[0]):
        place_ref[i] = map_near[ids_near[i]]
    for copy in large:
        copy.wait()
    pltpu.make_async_copy(grad_ref, rows, sems.at[4]).wait()


def score_kernel(slots, place_ref, saved_ref, grad_ref, rows_ref, *refs):
    memory, (terms_ref, sent_ref) = refs[:-2], refs[-2:]
    me = lax.axis_index("dp")
    section = lax.axis_index("pipe")
    tokens, width = saved_ref.shape
    heads = width // HEAD_DIM
    back = place_ref[1]
    behind, slot = lax.rem(me - back // slots + len(memory), len(memory)), back % slots
    keys = pick(memory, 0, behind, slot)
    values = pick(memory, slots, behind, slot)
    count = keys.shape[0]
    saved, grads = saved_ref[...], grad_ref[...]
    weights = softmax_t(keys, saved)
    grad_weights = per_head(values, grads)
    centre = jnp.sum(weights * grad_weights, axis=1, keepdims=True)
    grad_scores = weights * (grad_weights - centre) * (1.0 / math.sqrt(HEAD_DIM))
    flat = heads * count
    grad_scores = grad_scores.astype(jnp.bfloat16)
    terms_ref[:, :width] = reduced(grad_scores, saved).astype(jnp.bfloat16)
    terms_ref[:, width : 2 * width] = reduced(weights.astype(jnp.bfloat16), grads).astype(jnp.bfloat16)
    grad_scores = grad_scores.reshape(flat, tokens)
    place = jnp.full((count, HEAD_DIM), back, jnp.int32)
    terms_ref[:, 2 * width :] = place.astype(jnp.float32).astype(jnp.bfloat16)
    first, second = tokens, tokens + padded(count)

    @pl.when(section == 0)
    def _():
        ahead = place_ref[0]
        behind, slot = lax.rem(me - ahead // slots + len(memory), len(memory)), ahead % slots
        sent_ref[first : first + count, :] = pick(memory, 0, behind, slot)
        sent_ref[second : second + count, :] = pick(memory, slots, behind, slot)

    @pl.when(section != 0)
    def _():
        sent_ref[first : first + count, :] = keys
        part = flat * tokens // width
        for i in range(width // tokens):
            at = slice(i * tokens, (i + 1) * tokens)
            sent_ref[second : second + part, at] = grad_scores[i * part : (i + 1) * part, :]


def output_kernel(tokens, count, sent_ref, next_ref, back_ref):
    width = sent_ref.shape[1]
    heads = width // HEAD_DIM
    first, second = tokens, tokens + padded(count)
    keys = sent_ref[first : first + count, :]
    rows = sent_ref[:tokens, :]
    section = lax.axis_index("pipe")

    @pl.when(section == 0)
    def _():
        next_ref[...] = jnp.zeros_like(next_ref)
        part = heads * count * tokens // width
        grad_scores = [
            sent_ref[second : second + part, i * tokens : (i + 1) * tokens]
            for i in range(width // tokens)
        ]
        added = dot(jnp.concatenate(grad_scores, axis=0), by_head(keys), TN)
        back_ref[...] = (rows.astype(jnp.float32) + added).astype(jnp.bfloat16)

    @pl.when(section != 0)
    def _():
        back_ref[...] = jnp.zeros_like(back_ref)
        values = by_head(sent_ref[second : second + count, :])
        weights = softmax_t(keys, rows).astype(jnp.bfloat16).reshape(-1, tokens)
        added = dot(weights, values, TN)
        next_ref[...] = (rows.astype(jnp.float32) + added).astype(jnp.bfloat16)


def sum_kernel(slots, *refs):
    terms_refs, (key_ref, value_ref) = refs[:-2], refs[-2:]
    me = lax.axis_index("dp")
    width = key_ref.shape[2]
    tiles = width // HEAD_DIM
    terms = [ref[...].astype(jnp.float32) for ref in terms_refs]
    for slot in range(slots):
        here = (me * slots + slot).astype(jnp.float32)
        hits = [t[:, 2 * width :] == here for t in terms]
        for i in range(2 * tiles):
            at = slice(i * HEAD_DIM, (i + 1) * HEAD_DIM)
            total = sum(jnp.where(hit, t[:, at], 0.0) for hit, t in zip(hits, terms))
            out, j = (key_ref, i) if i < tiles else (value_ref, i - tiles)
            out[slot, :, j * HEAD_DIM : (j + 1) * HEAD_DIM] = total.astype(jnp.bfloat16)


def exchange(x, replicas):
    return [x] + [
        lax.ppermute(x, "dp", [(i, (i + d) % replicas) for i in range(replicas)])
        for d in range(replicas - 1, 0, -1)
    ]


def vmem(x):
    return pltpu.with_memory_space_constraint(x, pltpu.VMEM)


def hbm(x):
    return pltpu.with_memory_space_constraint(x, pltpu.HBM)


def smem(x):
    return pltpu.with_memory_space_constraint(x, pltpu.SMEM)


def call(kernel, name, out, in_specs, scratch=(), moved=0, aliases=()):
    return pl.pallas_call(
        kernel,
        out_shape=out,
        in_specs=in_specs,
        out_specs=jax.tree.map(lambda o: SMEM if o.shape == (2,) else VMEM, out),
        scratch_shapes=scratch,
        input_output_aliases=dict(aliases),
        compiler_params=pltpu.CompilerParams(vmem_limit_bytes=16 * 1024 * 1024),
        cost_estimate=pl.CostEstimate(flops=0, bytes_accessed=moved, transcendentals=0),
        name=name,
    )


def direct(stream_in, saved_in, grad_out, mem_keys, mem_values, owner_map, block_ids):
    replicas = lax.axis_size("dp")
    slots, block_rows, width = mem_keys.shape[1:]
    tokens = stream_in.shape[1]
    rows = pltpu.VMEM((tokens, width), jnp.bfloat16)
    grad_lines = width // HEAD_DIM * block_rows * tokens // width
    sent_rows = tokens + padded(block_rows) + padded(max(block_rows, grad_lines))
    sent = pltpu.VMEM((sent_rows, width), jnp.bfloat16)
    stacked = call(
        stack_kernel,
        "stack",
        pltpu.VMEM((2 * slots, block_rows, width), jnp.bfloat16),
        [HBM] * 2,
        [pltpu.SemaphoreType.DMA((2,))],
    )(hbm(mem_keys[0]), hbm(mem_values[0]))
    stacked, *own = lax.optimization_barrier(
        (stacked, owner_map, block_ids.reshape(-1), stream_in[0], saved_in[0], grad_out[0])
    )
    memory = exchange(stacked, replicas)
    saved, grads, to_send, places = call(
        fetch_kernel,
        "fetch",
        (rows, rows, sent, pltpu.SMEM((2,), jnp.int32)),
        [HBM] * 5,
        [
            pltpu.SMEM(owner_map.shape, jnp.int32),
            pltpu.SMEM((2,), jnp.int32),
            pltpu.SemaphoreType.DMA((5,)),
        ],
        12 * tokens * width,
    )(*map(hbm, own))
    terms, to_send = call(
        functools.partial(score_kernel, slots),
        "scores",
        (pltpu.VMEM((block_rows, 2 * width + HEAD_DIM), jnp.bfloat16), sent),
        [SMEM] + [VMEM] * (3 + replicas),
        aliases={3: 1}.items(),
    )(smem(places), *map(vmem, (saved, grads, to_send, *memory)))
    other_sent = lax.ppermute(to_send, "pipe", [(0, 1), (1, 0)])
    term_parts = exchange(terms, replicas)
    next_input, grad_back = call(
        functools.partial(output_kernel, tokens, block_rows),
        "outputs",
        (jax.ShapeDtypeStruct((tokens, width), jnp.bfloat16),) * 2,
        [VMEM],
        (),
        4 * tokens * width,
    )(vmem(other_sent))
    *term_parts, next_input, grad_back = lax.optimization_barrier((*term_parts, next_input, grad_back))
    key_grad, value_grad = call(
        functools.partial(sum_kernel, slots),
        "sums",
        (jax.ShapeDtypeStruct((slots, block_rows, width), jnp.bfloat16),) * 2,
        [VMEM] * replicas,
    )(*map(vmem, term_parts))
    return next_input[None], grad_back[None], key_grad[None], value_grad[None]


def from_behind(x, axis, by):
    peers = lax.axis_size(axis)
    pairs = [(i, i + by) for i in range(peers) if 0 <= i + by < peers]
    return lax.ppermute(x, axis, pairs)


def forward_part(inputs, memory_keys, memory_values):
    rows = inputs.shape[0]
    heads_count = inputs.shape[1] // HEAD_DIM
    scale = 1.0 / math.sqrt(HEAD_DIM)
    queries = inputs.reshape(rows, heads_count, HEAD_DIM)
    key_rows = memory_keys.reshape(-1, heads_count, HEAD_DIM)
    value_rows = memory_values.reshape(-1, heads_count, HEAD_DIM)
    scores = (
        jnp.einsum("thd,khd->htk", queries, key_rows, preferred_element_type=jnp.float32) * scale
    )
    exponent = jnp.exp(scores - jnp.max(scores, axis=-1, keepdims=True))
    weights = exponent / jnp.sum(exponent, axis=-1, keepdims=True)
    rounded = weights.astype(jnp.bfloat16)
    attended = jnp.einsum(
        "htk,khd->thd", rounded, value_rows, preferred_element_type=jnp.float32
    ).reshape(rows, -1)
    return (queries, key_rows, value_rows, weights, rounded, attended)


def backward_part(inputs, grads, memory_keys, memory_values):
    queries, key_rows, value_rows, weights, rounded, attended = forward_part(
        inputs, memory_keys, memory_values
    )
    rows = inputs.shape[0]
    heads_count = queries.shape[1]
    scale = 1.0 / math.sqrt(HEAD_DIM)
    grad_rows = grads.reshape(rows, heads_count, HEAD_DIM)
    grad_weights = jnp.einsum(
        "thd,khd->htk", grad_rows, value_rows, preferred_element_type=jnp.float32
    )
    centre = jnp.sum(weights * grad_weights, axis=-1, keepdims=True)
    grad_scores = (weights * (grad_weights - centre) * scale).astype(jnp.bfloat16)
    grad_queries = jnp.einsum(
        "htk,khd->thd", grad_scores, key_rows, preferred_element_type=jnp.float32
    ).reshape(rows, -1)
    key_terms = jnp.einsum("htk,thd->khd", grad_scores, queries, preferred_element_type=jnp.float32)
    value_terms = jnp.einsum("htk,thd->khd", rounded, grad_rows, preferred_element_type=jnp.float32)
    input_grad = (grads.astype(jnp.float32) + grad_queries).astype(jnp.bfloat16)
    key_count = key_rows.shape[0]
    return (
        input_grad,
        key_terms.reshape(key_count, -1).astype(jnp.bfloat16),
        value_terms.reshape(key_count, -1).astype(jnp.bfloat16),
    )


def routed(stream_in, saved_in, grad_out, mem_keys, mem_values, owner_map, block_ids):
    replicas = lax.axis_size("dp")
    local_blocks = mem_keys.shape[1]
    block_rows = mem_keys.shape[2]
    width = stream_in.shape[2]
    table_size = owner_map.shape[0]
    requested = block_ids.reshape(-1)
    picks = requested.shape[0]
    half = picks // 2
    matches = requested[:, None] == jnp.arange(table_size, dtype=jnp.int32)[None, :]
    places = jnp.sum(jnp.where(matches, owner_map[None, :], 0), axis=1)
    owners = places // local_blocks
    slot_ids = places % local_blocks
    owner_hits = owners[:, None] == jnp.arange(replicas, dtype=jnp.int32)[None, :]
    served = None
    wanted = jnp.sum(jnp.where(owner_hits, slot_ids[:, None], 0), axis=0)
    served = lax.all_to_all(
        wanted.reshape(replicas, 1), "dp", split_axis=0, concat_axis=0, tiled=True
    ).reshape(replicas)
    out_keys = jnp.take(mem_keys[0], served, axis=0)
    out_values = jnp.take(mem_values[0], served, axis=0)
    got_keys, got_values = (
        lax.all_to_all(out_keys, "dp", split_axis=0, concat_axis=0, tiled=True),
        lax.all_to_all(out_values, "dp", split_axis=0, concat_axis=0, tiled=True),
    )
    fetched_keys = jnp.take(got_keys, owners, axis=0)
    fetched_values = jnp.take(got_values, owners, axis=0)
    forward_keys = fetched_keys[:half].reshape(-1, width)
    forward_values = fetched_values[:half].reshape(-1, width)
    backward_keys = fetched_keys[half:].reshape(-1, width)
    backward_values = fetched_values[half:].reshape(-1, width)
    attended = forward_part(stream_in[0], forward_keys, forward_values)[5]
    section_out = (stream_in[0].astype(jnp.float32) + attended).astype(jnp.bfloat16)
    next_input = from_behind(section_out[None], "pipe", 1)
    input_grad, key_terms, value_terms = backward_part(
        saved_in[0], grad_out[0], backward_keys, backward_values
    )
    grad_back = from_behind(input_grad[None], "pipe", -1)
    key_blocks = key_terms.reshape(half, block_rows, width)
    value_blocks = value_terms.reshape(half, block_rows, width)
    back_hits = owner_hits[half:].astype(jnp.bfloat16)
    send_keys = jnp.einsum(
        "ro,rtf->otf", back_hits, key_blocks, preferred_element_type=jnp.float32
    ).astype(jnp.bfloat16)
    send_values = jnp.einsum(
        "ro,rtf->otf", back_hits, value_blocks, preferred_element_type=jnp.float32
    ).astype(jnp.bfloat16)
    recv_keys, recv_values = (
        lax.all_to_all(send_keys, "dp", split_axis=0, concat_axis=0, tiled=True),
        lax.all_to_all(send_values, "dp", split_axis=0, concat_axis=0, tiled=True),
    )
    slot_hits = (served[:, None] == jnp.arange(local_blocks, dtype=jnp.int32)[None, :]).astype(
        jnp.bfloat16
    )
    key_grad = jnp.einsum(
        "sm,stf->mtf", slot_hits, recv_keys, preferred_element_type=jnp.float32
    ).astype(jnp.bfloat16)
    value_grad = jnp.einsum(
        "sm,stf->mtf", slot_hits, recv_values, preferred_element_type=jnp.float32
    ).astype(jnp.bfloat16)
    return (next_input, grad_back, key_grad[None], value_grad[None])


def local(*args):
    replicas, (_, tokens, width) = lax.axis_size("dp"), args[0].shape
    few = replicas <= DIRECT_REPLICAS
    one_each = args[-1].size == 2 and lax.axis_size("pipe") == 2 and width % tokens == 0
    return (direct if few and one_each else routed)(*args)


def solution(mesh):
    in_specs = (
        P("pipe", "dp", "tensor"),
        P("pipe", "dp", "tensor"),
        P("pipe", "dp", "tensor"),
        P("pipe", "dp", None, "tensor"),
        P("pipe", "dp", None, "tensor"),
        P(),
        P(None, "pipe", "dp", None),
    )
    out_specs = (
        P("pipe", "dp", "tensor"),
        P("pipe", "dp", "tensor"),
        P("pipe", "dp", None, "tensor"),
        P("pipe", "dp", None, "tensor"),
    )
    return jax.shard_map(local, mesh=mesh, in_specs=in_specs, out_specs=out_specs, check_vma=False)
```

```python
import functools
import math

import jax
import jax.numpy as jnp
from jax import lax
from jax.experimental import pallas as pl
from jax.experimental.pallas import tpu as pltpu
from jax.sharding import PartitionSpec as P

HEAD_DIM = 128
DIRECT_REPLICAS = 8
HBM = pl.BlockSpec(memory_space=pltpu.HBM)
VMEM = pl.BlockSpec(memory_space=pltpu.VMEM)
SMEM = pl.BlockSpec(memory_space=pltpu.SMEM)
NT = (((1,), (1,)), ((), ()))
NN = (((1,), (0,)), ((), ()))
TN = (((0,), (0,)), ((), ()))


def padded(rows):
    return -(-rows // 16) * 16


def dot(a, b, dims):
    return lax.dot_general(a, b, dims, preferred_element_type=jnp.float32)


def by_head(block):
    keys, width = block.shape
    heads = width // HEAD_DIM
    wide = jnp.broadcast_to(block.astype(jnp.float32)[None], (heads, keys, width))
    head = lax.broadcasted_iota(jnp.int32, wide.shape, 0)
    feature_head = lax.broadcasted_iota(jnp.int32, wide.shape, 2) // HEAD_DIM
    return jnp.where(head == feature_head, wide, 0.0).reshape(heads * keys, width).astype(block.dtype)


def groups(width):
    step = min(width, 2 * HEAD_DIM)
    return [slice(i, i + step) for i in range(0, width, step)]


def per_head(block, rows):
    parts = [dot(by_head(block[:, at]), rows[:, at], NT) for at in groups(rows.shape[1])]
    return jnp.concatenate(parts, axis=0).reshape(-1, block.shape[0], rows.shape[0])


def reduced(by_key, rows):
    keys, tokens = by_key.shape[1:]
    parts = []
    for at in groups(rows.shape[1]):
        heads = slice(at.start // HEAD_DIM, at.stop // HEAD_DIM)
        product = dot(by_key[heads].reshape(-1, tokens), rows[:, at], NN)
        parts += [
            product[h * keys : (h + 1) * keys, h * HEAD_DIM : (h + 1) * HEAD_DIM]
            for h in range(heads.stop - heads.start)
        ]
    return jnp.concatenate(parts, axis=1)


def softmax_t(keys, rows):
    scores = per_head(keys, rows) * (1.0 / math.sqrt(HEAD_DIM))
    exponent = jnp.exp(scores - jnp.max(scores, axis=1, keepdims=True))
    return exponent / jnp.sum(exponent, axis=1, keepdims=True)


def pick(refs, first, behind, slot):
    block = refs[0][first + slot]
    for i in range(1, len(refs)):
        block = jnp.where(behind == len(refs) - i, refs[i][first + slot], block)
    return block


def stack_kernel(keys_ref, values_ref, out_ref, sems):
    slots = keys_ref.shape[0]
    copies = [
        pltpu.make_async_copy(keys_ref, out_ref.at[:slots], sems.at[0]),
        pltpu.make_async_copy(values_ref, out_ref.at[slots:], sems.at[1]),
    ]
    for copy in copies:
        copy.start()
    for copy in copies:
        copy.wait()


def fetch_kernel(map_ref, ids_ref, stream_ref, saved_ref, grad_ref, *refs):
    saved_near, grad_near, sent_ref, place_ref, map_near, ids_near, sems = refs
    rows = sent_ref.at[: stream_ref.shape[0]]
    section = lax.axis_index("pipe")
    small = [
        pltpu.make_async_copy(map_ref, map_near, sems.at[0]),
        pltpu.make_async_copy(ids_ref, ids_near, sems.at[1]),
    ]
    large = [
        pltpu.make_async_copy(saved_ref, saved_near, sems.at[2]),
        pltpu.make_async_copy(grad_ref, grad_near, sems.at[3]),
    ]
    for copy in small + large:
        copy.start()

    @pl.when(section == 0)
    def _():
        pltpu.make_async_copy(stream_ref, rows, sems.at[4]).start()

    @pl.when(section != 0)
    def _():
        pltpu.make_async_copy(grad_ref, rows, sems.at[4]).start()

    for copy in small:
        copy.wait()
    for i in range(place_ref.shape[0]):
        place_ref[i] = map_near[ids_near[i]]
    for copy in large:
        copy.wait()
    pltpu.make_async_copy(grad_ref, rows, sems.at[4]).wait()


def score_kernel(slots, place_ref, saved_ref, grad_ref, rows_ref, *refs):
    memory, (terms_ref, sent_ref) = refs[:-2], refs[-2:]
    me = lax.axis_index("dp")
    section = lax.axis_index("pipe")
    tokens, width = saved_ref.shape
    heads = width // HEAD_DIM
    back = place_ref[1]
    behind, slot = lax.rem(me - back // slots + len(memory), len(memory)), back % slots
    keys = pick(memory, 0, behind, slot)
    values = pick(memory, slots, behind, slot)
    count = keys.shape[0]
    first, second = tokens, tokens + padded(count)

    @pl.when(section == 0)
    def _():
        ahead = place_ref[0]
        behind, slot = lax.rem(me - ahead // slots + len(memory), len(memory)), ahead % slots
        sent_ref[first : first + count, :] = pick(memory, 0, behind, slot)
        sent_ref[second : second + count, :] = pick(memory, slots, behind, slot)

    saved, grads = saved_ref[...], grad_ref[...]
    weights = softmax_t(keys, saved)
    grad_weights = per_head(values, grads)
    centre = jnp.sum(weights * grad_weights, axis=1, keepdims=True)
    grad_scores = weights * (grad_weights - centre) * (1.0 / math.sqrt(HEAD_DIM))
    flat = heads * count
    grad_scores = grad_scores.astype(jnp.bfloat16)
    terms_ref[:, :width] = reduced(grad_scores, saved).astype(jnp.bfloat16)
    terms_ref[:, width : 2 * width] = reduced(weights.astype(jnp.bfloat16), grads).astype(jnp.bfloat16)
    grad_scores = grad_scores.reshape(flat, tokens)
    place = jnp.full((count, HEAD_DIM), back, jnp.int32)
    terms_ref[:, 2 * width :] = place.astype(jnp.float32).astype(jnp.bfloat16)
    @pl.when(section != 0)
    def _():
        sent_ref[first : first + count, :] = keys
        part = flat * tokens // width
        for i in range(width // tokens):
            at = slice(i * tokens, (i + 1) * tokens)
            sent_ref[second : second + part, at] = grad_scores[i * part : (i + 1) * part, :]


def output_kernel(tokens, count, sent_ref, next_ref, back_ref):
    width = sent_ref.shape[1]
    heads = width // HEAD_DIM
    first, second = tokens, tokens + padded(count)
    keys = sent_ref[first : first + count, :]
    rows = sent_ref[:tokens, :]
    section = lax.axis_index("pipe")

    @pl.when(section == 0)
    def _():
        next_ref[...] = jnp.zeros_like(next_ref)
        part = heads * count * tokens // width
        grad_scores = [
            sent_ref[second : second + part, i * tokens : (i + 1) * tokens]
            for i in range(width // tokens)
        ]
        added = dot(jnp.concatenate(grad_scores, axis=0), by_head(keys), TN)
        back_ref[...] = (rows.astype(jnp.float32) + added).astype(jnp.bfloat16)

    @pl.when(section != 0)
    def _():
        back_ref[...] = jnp.zeros_like(back_ref)
        values = by_head(sent_ref[second : second + count, :])
        weights = softmax_t(keys, rows).astype(jnp.bfloat16).reshape(-1, tokens)
        added = dot(weights, values, TN)
        next_ref[...] = (rows.astype(jnp.float32) + added).astype(jnp.bfloat16)


def sum_kernel(slots, *refs):
    terms_refs, (key_ref, value_ref) = refs[:-2], refs[-2:]
    me = lax.axis_index("dp")
    width = key_ref.shape[2]
    tiles = width // HEAD_DIM
    terms = [ref[...].astype(jnp.float32) for ref in terms_refs]
    for slot in range(slots):
        here = (me * slots + slot).astype(jnp.float32)
        hits = [t[:, 2 * width :] == here for t in terms]
        for i in range(2 * tiles):
            at = slice(i * HEAD_DIM, (i + 1) * HEAD_DIM)
            total = sum(jnp.where(hit, t[:, at], 0.0) for hit, t in zip(hits, terms))
            out, j = (key_ref, i) if i < tiles else (value_ref, i - tiles)
            out[slot, :, j * HEAD_DIM : (j + 1) * HEAD_DIM] = total.astype(jnp.bfloat16)


def exchange(x, replicas):
    return [x] + [
        lax.ppermute(x, "dp", [(i, (i + d) % replicas) for i in range(replicas)])
        for d in range(replicas - 1, 0, -1)
    ]


def vmem(x):
    return pltpu.with_memory_space_constraint(x, pltpu.VMEM)


def hbm(x):
    return pltpu.with_memory_space_constraint(x, pltpu.HBM)


def smem(x):
    return pltpu.with_memory_space_constraint(x, pltpu.SMEM)


def call(kernel, name, out, in_specs, scratch=(), moved=0, aliases=()):
    return pl.pallas_call(
        kernel,
        out_shape=out,
        in_specs=in_specs,
        out_specs=jax.tree.map(lambda o: SMEM if o.shape == (2,) else VMEM, out),
        scratch_shapes=scratch,
        input_output_aliases=dict(aliases),
        compiler_params=pltpu.CompilerParams(vmem_limit_bytes=16 * 1024 * 1024),
        cost_estimate=pl.CostEstimate(flops=0, bytes_accessed=moved, transcendentals=0),
        name=name,
    )


def direct(stream_in, saved_in, grad_out, mem_keys, mem_values, owner_map, block_ids):
    replicas = lax.axis_size("dp")
    slots, block_rows, width = mem_keys.shape[1:]
    tokens = stream_in.shape[1]
    rows = pltpu.VMEM((tokens, width), jnp.bfloat16)
    grad_lines = width // HEAD_DIM * block_rows * tokens // width
    sent_rows = tokens + padded(block_rows) + padded(max(block_rows, grad_lines))
    sent = pltpu.VMEM((sent_rows, width), jnp.bfloat16)
    stacked = call(
        stack_kernel,
        "stack",
        pltpu.VMEM((2 * slots, block_rows, width), jnp.bfloat16),
        [HBM] * 2,
        [pltpu.SemaphoreType.DMA((2,))],
    )(hbm(mem_keys[0]), hbm(mem_values[0]))
    stacked, *own = lax.optimization_barrier(
        (stacked, owner_map, block_ids.reshape(-1), stream_in[0], saved_in[0], grad_out[0])
    )
    memory = exchange(stacked, replicas)
    saved, grads, to_send, places = call(
        fetch_kernel,
        "fetch",
        (rows, rows, sent, pltpu.SMEM((2,), jnp.int32)),
        [HBM] * 5,
        [
            pltpu.SMEM(owner_map.shape, jnp.int32),
            pltpu.SMEM((2,), jnp.int32),
            pltpu.SemaphoreType.DMA((5,)),
        ],
        12 * tokens * width,
    )(*map(hbm, own))
    terms, to_send = call(
        functools.partial(score_kernel, slots),
        "scores",
        (pltpu.VMEM((block_rows, 2 * width + HEAD_DIM), jnp.bfloat16), sent),
        [SMEM] + [VMEM] * (3 + replicas),
        aliases={3: 1}.items(),
    )(smem(places), *map(vmem, (saved, grads, to_send, *memory)))
    other_sent = lax.ppermute(to_send, "pipe", [(0, 1), (1, 0)])
    term_parts = exchange(terms, replicas)
    next_input, grad_back = call(
        functools.partial(output_kernel, tokens, block_rows),
        "outputs",
        (jax.ShapeDtypeStruct((tokens, width), jnp.bfloat16),) * 2,
        [VMEM],
        (),
        4 * tokens * width,
    )(vmem(other_sent))
    *term_parts, next_input, grad_back = lax.optimization_barrier((*term_parts, next_input, grad_back))
    key_grad, value_grad = call(
        functools.partial(sum_kernel, slots),
        "sums",
        (jax.ShapeDtypeStruct((slots, block_rows, width), jnp.bfloat16),) * 2,
        [VMEM] * replicas,
    )(*map(vmem, term_parts))
    return next_input[None], grad_back[None], key_grad[None], value_grad[None]


def from_behind(x, axis, by):
    peers = lax.axis_size(axis)
    pairs = [(i, i + by) for i in range(peers) if 0 <= i + by < peers]
    return lax.ppermute(x, axis, pairs)


def forward_part(inputs, memory_keys, memory_values):
    rows = inputs.shape[0]
    heads_count = inputs.shape[1] // HEAD_DIM
    scale = 1.0 / math.sqrt(HEAD_DIM)
    queries = inputs.reshape(rows, heads_count, HEAD_DIM)
    key_rows = memory_keys.reshape(-1, heads_count, HEAD_DIM)
    value_rows = memory_values.reshape(-1, heads_count, HEAD_DIM)
    scores = (
        jnp.einsum("thd,khd->htk", queries, key_rows, preferred_element_type=jnp.float32) * scale
    )
    exponent = jnp.exp(scores - jnp.max(scores, axis=-1, keepdims=True))
    weights = exponent / jnp.sum(exponent, axis=-1, keepdims=True)
    rounded = weights.astype(jnp.bfloat16)
    attended = jnp.einsum(
        "htk,khd->thd", rounded, value_rows, preferred_element_type=jnp.float32
    ).reshape(rows, -1)
    return (queries, key_rows, value_rows, weights, rounded, attended)


def backward_part(inputs, grads, memory_keys, memory_values):
    queries, key_rows, value_rows, weights, rounded, attended = forward_part(
        inputs, memory_keys, memory_values
    )
    rows = inputs.shape[0]
    heads_count = queries.shape[1]
    scale = 1.0 / math.sqrt(HEAD_DIM)
    grad_rows = grads.reshape(rows, heads_count, HEAD_DIM)
    grad_weights = jnp.einsum(
        "thd,khd->htk", grad_rows, value_rows, preferred_element_type=jnp.float32
    )
    centre = jnp.sum(weights * grad_weights, axis=-1, keepdims=True)
    grad_scores = (weights * (grad_weights - centre) * scale).astype(jnp.bfloat16)
    grad_queries = jnp.einsum(
        "htk,khd->thd", grad_scores, key_rows, preferred_element_type=jnp.float32
    ).reshape(rows, -1)
    key_terms = jnp.einsum("htk,thd->khd", grad_scores, queries, preferred_element_type=jnp.float32)
    value_terms = jnp.einsum("htk,thd->khd", rounded, grad_rows, preferred_element_type=jnp.float32)
    input_grad = (grads.astype(jnp.float32) + grad_queries).astype(jnp.bfloat16)
    key_count = key_rows.shape[0]
    return (
        input_grad,
        key_terms.reshape(key_count, -1).astype(jnp.bfloat16),
        value_terms.reshape(key_count, -1).astype(jnp.bfloat16),
    )


def routed(stream_in, saved_in, grad_out, mem_keys, mem_values, owner_map, block_ids):
    replicas = lax.axis_size("dp")
    local_blocks = mem_keys.shape[1]
    block_rows = mem_keys.shape[2]
    width = stream_in.shape[2]
    table_size = owner_map.shape[0]
    requested = block_ids.reshape(-1)
    picks = requested.shape[0]
    half = picks // 2
    matches = requested[:, None] == jnp.arange(table_size, dtype=jnp.int32)[None, :]
    places = jnp.sum(jnp.where(matches, owner_map[None, :], 0), axis=1)
    owners = places // local_blocks
    slot_ids = places % local_blocks
    owner_hits = owners[:, None] == jnp.arange(replicas, dtype=jnp.int32)[None, :]
    served = None
    wanted = jnp.sum(jnp.where(owner_hits, slot_ids[:, None], 0), axis=0)
    served = lax.all_to_all(
        wanted.reshape(replicas, 1), "dp", split_axis=0, concat_axis=0, tiled=True
    ).reshape(replicas)
    out_keys = jnp.take(mem_keys[0], served, axis=0)
    out_values = jnp.take(mem_values[0], served, axis=0)
    got_keys, got_values = (
        lax.all_to_all(out_keys, "dp", split_axis=0, concat_axis=0, tiled=True),
        lax.all_to_all(out_values, "dp", split_axis=0, concat_axis=0, tiled=True),
    )
    fetched_keys = jnp.take(got_keys, owners, axis=0)
    fetched_values = jnp.take(got_values, owners, axis=0)
    forward_keys = fetched_keys[:half].reshape(-1, width)
    forward_values = fetched_values[:half].reshape(-1, width)
    backward_keys = fetched_keys[half:].reshape(-1, width)
    backward_values = fetched_values[half:].reshape(-1, width)
    attended = forward_part(stream_in[0], forward_keys, forward_values)[5]
    section_out = (stream_in[0].astype(jnp.float32) + attended).astype(jnp.bfloat16)
    next_input = from_behind(section_out[None], "pipe", 1)
    input_grad, key_terms, value_terms = backward_part(
        saved_in[0], grad_out[0], backward_keys, backward_values
    )
    grad_back = from_behind(input_grad[None], "pipe", -1)
    key_blocks = key_terms.reshape(half, block_rows, width)
    value_blocks = value_terms.reshape(half, block_rows, width)
    back_hits = owner_hits[half:].astype(jnp.bfloat16)
    send_keys = jnp.einsum(
        "ro,rtf->otf", back_hits, key_blocks, preferred_element_type=jnp.float32
    ).astype(jnp.bfloat16)
    send_values = jnp.einsum(
        "ro,rtf->otf", back_hits, value_blocks, preferred_element_type=jnp.float32
    ).astype(jnp.bfloat16)
    recv_keys, recv_values = (
        lax.all_to_all(send_keys, "dp", split_axis=0, concat_axis=0, tiled=True),
        lax.all_to_all(send_values, "dp", split_axis=0, concat_axis=0, tiled=True),
    )
    slot_hits = (served[:, None] == jnp.arange(local_blocks, dtype=jnp.int32)[None, :]).astype(
        jnp.bfloat16
    )
    key_grad = jnp.einsum(
        "sm,stf->mtf", slot_hits, recv_keys, preferred_element_type=jnp.float32
    ).astype(jnp.bfloat16)
    value_grad = jnp.einsum(
        "sm,stf->mtf", slot_hits, recv_values, preferred_element_type=jnp.float32
    ).astype(jnp.bfloat16)
    return (next_input, grad_back, key_grad[None], value_grad[None])


def local(*args):
    replicas, (_, tokens, width) = lax.axis_size("dp"), args[0].shape
    few = replicas <= DIRECT_REPLICAS
    one_each = args[-1].size == 2 and lax.axis_size("pipe") == 2 and width % tokens == 0
    small = args[-2].size <= 256
    return (direct if few and one_each and small else routed)(*args)


def solution(mesh):
    in_specs = (
        P("pipe", "dp", "tensor"),
        P("pipe", "dp", "tensor"),
        P("pipe", "dp", "tensor"),
        P("pipe", "dp", None, "tensor"),
        P("pipe", "dp", None, "tensor"),
        P(),
        P(None, "pipe", "dp", None),
    )
    out_specs = (
        P("pipe", "dp", "tensor"),
        P("pipe", "dp", "tensor"),
        P("pipe", "dp", None, "tensor"),
        P("pipe", "dp", None, "tensor"),
    )
    return jax.shard_map(local, mesh=mesh, in_specs=in_specs, out_specs=out_specs, check_vma=False)
```

```python
import functools
import math

import jax
import jax.numpy as jnp
from jax import lax
from jax.experimental import pallas as pl
from jax.experimental.pallas import tpu as pltpu
from jax.sharding import PartitionSpec as P

HEAD_DIM = 128
DIRECT_REPLICAS = 8
SEND = ((2, 0, 3, 1), (3, 2, 1, 0), (1, 3, 0, 2))
HBM = pl.BlockSpec(memory_space=pltpu.HBM)
VMEM = pl.BlockSpec(memory_space=pltpu.VMEM)
SMEM = pl.BlockSpec(memory_space=pltpu.SMEM)
NT = (((1,), (1,)), ((), ()))
NN = (((1,), (0,)), ((), ()))
TN = (((0,), (0,)), ((), ()))


def padded(rows):
    return -(-rows // 16) * 16


def dot(a, b, dims):
    return lax.dot_general(a, b, dims, preferred_element_type=jnp.float32)


def by_head(block):
    keys, width = block.shape
    heads = width // HEAD_DIM
    wide = jnp.broadcast_to(block.astype(jnp.float32)[None], (heads, keys, width))
    head = lax.broadcasted_iota(jnp.int32, wide.shape, 0)
    feature_head = lax.broadcasted_iota(jnp.int32, wide.shape, 2) // HEAD_DIM
    return jnp.where(head == feature_head, wide, 0.0).reshape(heads * keys, width).astype(block.dtype)


def groups(width):
    step = min(width, 2 * HEAD_DIM)
    return [slice(i, i + step) for i in range(0, width, step)]


def per_head(block, rows):
    parts = [dot(by_head(block[:, at]), rows[:, at], NT) for at in groups(rows.shape[1])]
    return jnp.concatenate(parts, axis=0).reshape(-1, block.shape[0], rows.shape[0])


def reduced(by_key, rows):
    keys, tokens = by_key.shape[1:]
    parts = []
    for at in groups(rows.shape[1]):
        heads = slice(at.start // HEAD_DIM, at.stop // HEAD_DIM)
        product = dot(by_key[heads].reshape(-1, tokens), rows[:, at], NN)
        parts += [
            product[h * keys : (h + 1) * keys, h * HEAD_DIM : (h + 1) * HEAD_DIM]
            for h in range(heads.stop - heads.start)
        ]
    return jnp.concatenate(parts, axis=1)


def softmax_t(keys, rows):
    scores = per_head(keys, rows) * (1.0 / math.sqrt(HEAD_DIM))
    exponent = jnp.exp(scores - jnp.max(scores, axis=1, keepdims=True))
    return exponent / jnp.sum(exponent, axis=1, keepdims=True)


def pick(refs, first, behind, slot):
    block = refs[0][first + slot]
    for i in range(1, len(refs)):
        block = jnp.where(behind == len(refs) - i, refs[i][first + slot], block)
    return block


def stack_kernel(keys_ref, values_ref, out_ref, sems):
    slots = keys_ref.shape[0]
    copies = [
        pltpu.make_async_copy(keys_ref, out_ref.at[:slots], sems.at[0]),
        pltpu.make_async_copy(values_ref, out_ref.at[slots:], sems.at[1]),
    ]
    for copy in copies:
        copy.start()
    for copy in copies:
        copy.wait()


def fetch_kernel(map_ref, ids_ref, stream_ref, saved_ref, grad_ref, *refs):
    saved_near, grad_near, sent_ref, place_ref, map_near, ids_near, sems = refs
    rows = sent_ref.at[: stream_ref.shape[0]]
    section = lax.axis_index("pipe")
    small = [
        pltpu.make_async_copy(map_ref, map_near, sems.at[0]),
        pltpu.make_async_copy(ids_ref, ids_near, sems.at[1]),
    ]
    large = [
        pltpu.make_async_copy(saved_ref, saved_near, sems.at[2]),
        pltpu.make_async_copy(grad_ref, grad_near, sems.at[3]),
    ]
    for copy in small + large:
        copy.start()

    @pl.when(section == 0)
    def _():
        pltpu.make_async_copy(stream_ref, rows, sems.at[4]).start()

    @pl.when(section != 0)
    def _():
        pltpu.make_async_copy(grad_ref, rows, sems.at[4]).start()

    for copy in small:
        copy.wait()
    for i in range(place_ref.shape[0]):
        place_ref[i] = map_near[ids_near[i]]
    for copy in large:
        copy.wait()
    pltpu.make_async_copy(grad_ref, rows, sems.at[4]).wait()


def score_kernel(slots, place_ref, saved_ref, grad_ref, rows_ref, *refs):
    memory, (terms_ref, sent_ref) = refs[:-2], refs[-2:]
    me = lax.axis_index("dp")
    section = lax.axis_index("pipe")
    tokens, width = saved_ref.shape
    heads = width // HEAD_DIM
    back = place_ref[1]
    behind, slot = lax.rem(me - back // slots + len(memory), len(memory)), back % slots
    keys = pick(memory, 0, behind, slot)
    values = pick(memory, slots, behind, slot)
    count = keys.shape[0]
    first, second = tokens, tokens + padded(count)

    @pl.when(section == 0)
    def _():
        ahead = place_ref[0]
        behind, slot = lax.rem(me - ahead // slots + len(memory), len(memory)), ahead % slots
        sent_ref[first : first + count, :] = pick(memory, 0, behind, slot)
        sent_ref[second : second + count, :] = pick(memory, slots, behind, slot)

    saved, grads = saved_ref[...], grad_ref[...]
    weights = softmax_t(keys, saved)
    grad_weights = per_head(values, grads)
    centre = jnp.sum(weights * grad_weights, axis=1, keepdims=True)
    grad_scores = weights * (grad_weights - centre) * (1.0 / math.sqrt(HEAD_DIM))
    flat = heads * count
    grad_scores = grad_scores.astype(jnp.bfloat16)
    terms_ref[:, :width] = reduced(grad_scores, saved).astype(jnp.bfloat16)
    terms_ref[:, width : 2 * width] = reduced(weights.astype(jnp.bfloat16), grads).astype(jnp.bfloat16)
    grad_scores = grad_scores.reshape(flat, tokens)
    place = jnp.full((count, HEAD_DIM), back, jnp.int32)
    terms_ref[:, 2 * width :] = place.astype(jnp.float32).astype(jnp.bfloat16)
    @pl.when(section != 0)
    def _():
        sent_ref[first : first + count, :] = keys
        part = flat * tokens // width
        for i in range(width // tokens):
            at = slice(i * tokens, (i + 1) * tokens)
            sent_ref[second : second + part, at] = grad_scores[i * part : (i + 1) * part, :]


def output_kernel(tokens, count, sent_ref, next_ref, back_ref):
    width = sent_ref.shape[1]
    heads = width // HEAD_DIM
    first, second = tokens, tokens + padded(count)
    keys = sent_ref[first : first + count, :]
    rows = sent_ref[:tokens, :]
    section = lax.axis_index("pipe")

    @pl.when(section == 0)
    def _():
        next_ref[...] = jnp.zeros_like(next_ref)
        part = heads * count * tokens // width
        grad_scores = [
            sent_ref[second : second + part, i * tokens : (i + 1) * tokens]
            for i in range(width // tokens)
        ]
        added = dot(jnp.concatenate(grad_scores, axis=0), by_head(keys), TN)
        back_ref[...] = (rows.astype(jnp.float32) + added).astype(jnp.bfloat16)

    @pl.when(section != 0)
    def _():
        back_ref[...] = jnp.zeros_like(back_ref)
        values = by_head(sent_ref[second : second + count, :])
        weights = softmax_t(keys, rows).astype(jnp.bfloat16).reshape(-1, tokens)
        added = dot(weights, values, TN)
        next_ref[...] = (rows.astype(jnp.float32) + added).astype(jnp.bfloat16)


def sum_kernel(slots, *refs):
    terms_refs, (key_ref, value_ref) = refs[:-2], refs[-2:]
    me = lax.axis_index("dp")
    width = key_ref.shape[2]
    tiles = width // HEAD_DIM
    terms = [ref[...].astype(jnp.float32) for ref in terms_refs]
    for slot in range(slots):
        here = (me * slots + slot).astype(jnp.float32)
        hits = [t[:, 2 * width :] == here for t in terms]
        for i in range(2 * tiles):
            at = slice(i * HEAD_DIM, (i + 1) * HEAD_DIM)
            total = sum(jnp.where(hit, t[:, at], 0.0) for hit, t in zip(hits, terms))
            out, j = (key_ref, i) if i < tiles else (value_ref, i - tiles)
            out[slot, :, j * HEAD_DIM : (j + 1) * HEAD_DIM] = total.astype(jnp.bfloat16)


def exchange(x, replicas, patterns=None):
    shifts = [[(i + d) % replicas for i in range(replicas)] for d in range(replicas - 1, 0, -1)]
    return [x] + [lax.ppermute(x, "dp", list(enumerate(p))) for p in patterns or shifts]


def vmem(x):
    return pltpu.with_memory_space_constraint(x, pltpu.VMEM)


def hbm(x):
    return pltpu.with_memory_space_constraint(x, pltpu.HBM)


def smem(x):
    return pltpu.with_memory_space_constraint(x, pltpu.SMEM)


def call(kernel, name, out, in_specs, scratch=(), moved=0, aliases=()):
    return pl.pallas_call(
        kernel,
        out_shape=out,
        in_specs=in_specs,
        out_specs=jax.tree.map(lambda o: SMEM if o.shape == (2,) else VMEM, out),
        scratch_shapes=scratch,
        input_output_aliases=dict(aliases),
        compiler_params=pltpu.CompilerParams(vmem_limit_bytes=16 * 1024 * 1024),
        cost_estimate=pl.CostEstimate(flops=0, bytes_accessed=moved, transcendentals=0),
        name=name,
    )


def direct(stream_in, saved_in, grad_out, mem_keys, mem_values, owner_map, block_ids):
    replicas = lax.axis_size("dp")
    slots, block_rows, width = mem_keys.shape[1:]
    tokens = stream_in.shape[1]
    rows = pltpu.VMEM((tokens, width), jnp.bfloat16)
    grad_lines = width // HEAD_DIM * block_rows * tokens // width
    sent_rows = tokens + padded(block_rows) + padded(max(block_rows, grad_lines))
    sent = pltpu.VMEM((sent_rows, width), jnp.bfloat16)
    stacked = call(
        stack_kernel,
        "stack",
        pltpu.VMEM((2 * slots, block_rows, width), jnp.bfloat16),
        [HBM] * 2,
        [pltpu.SemaphoreType.DMA((2,))],
    )(hbm(mem_keys[0]), hbm(mem_values[0]))
    stacked, *own = lax.optimization_barrier(
        (stacked, owner_map, block_ids.reshape(-1), stream_in[0], saved_in[0], grad_out[0])
    )
    memory = exchange(stacked, replicas)
    saved, grads, to_send, places = call(
        fetch_kernel,
        "fetch",
        (rows, rows, sent, pltpu.SMEM((2,), jnp.int32)),
        [HBM] * 5,
        [
            pltpu.SMEM(owner_map.shape, jnp.int32),
            pltpu.SMEM((2,), jnp.int32),
            pltpu.SemaphoreType.DMA((5,)),
        ],
        12 * tokens * width,
    )(*map(hbm, own))
    terms, to_send = call(
        functools.partial(score_kernel, slots),
        "scores",
        (pltpu.VMEM((block_rows, 2 * width + HEAD_DIM), jnp.bfloat16), sent),
        [SMEM] + [VMEM] * (3 + replicas),
        aliases={3: 1}.items(),
    )(smem(places), *map(vmem, (saved, grads, to_send, *memory)))
    other_sent = lax.ppermute(to_send, "pipe", [(0, 1), (1, 0)])
    term_parts = exchange(terms, replicas, SEND if replicas == 4 else None)
    next_input, grad_back = call(
        functools.partial(output_kernel, tokens, block_rows),
        "outputs",
        (jax.ShapeDtypeStruct((tokens, width), jnp.bfloat16),) * 2,
        [VMEM],
        (),
        4 * tokens * width,
    )(vmem(other_sent))
    *term_parts, next_input, grad_back = lax.optimization_barrier((*term_parts, next_input, grad_back))
    key_grad, value_grad = call(
        functools.partial(sum_kernel, slots),
        "sums",
        (jax.ShapeDtypeStruct((slots, block_rows, width), jnp.bfloat16),) * 2,
        [VMEM] * replicas,
    )(*map(vmem, term_parts))
    return next_input[None], grad_back[None], key_grad[None], value_grad[None]


def from_behind(x, axis, by):
    peers = lax.axis_size(axis)
    pairs = [(i, i + by) for i in range(peers) if 0 <= i + by < peers]
    return lax.ppermute(x, axis, pairs)


def forward_part(inputs, memory_keys, memory_values):
    rows = inputs.shape[0]
    heads_count = inputs.shape[1] // HEAD_DIM
    scale = 1.0 / math.sqrt(HEAD_DIM)
    queries = inputs.reshape(rows, heads_count, HEAD_DIM)
    key_rows = memory_keys.reshape(-1, heads_count, HEAD_DIM)
    value_rows = memory_values.reshape(-1, heads_count, HEAD_DIM)
    scores = (
        jnp.einsum("thd,khd->htk", queries, key_rows, preferred_element_type=jnp.float32) * scale
    )
    exponent = jnp.exp(scores - jnp.max(scores, axis=-1, keepdims=True))
    weights = exponent / jnp.sum(exponent, axis=-1, keepdims=True)
    rounded = weights.astype(jnp.bfloat16)
    attended = jnp.einsum(
        "htk,khd->thd", rounded, value_rows, preferred_element_type=jnp.float32
    ).reshape(rows, -1)
    return (queries, key_rows, value_rows, weights, rounded, attended)


def backward_part(inputs, grads, memory_keys, memory_values):
    queries, key_rows, value_rows, weights, rounded, attended = forward_part(
        inputs, memory_keys, memory_values
    )
    rows = inputs.shape[0]
    heads_count = queries.shape[1]
    scale = 1.0 / math.sqrt(HEAD_DIM)
    grad_rows = grads.reshape(rows, heads_count, HEAD_DIM)
    grad_weights = jnp.einsum(
        "thd,khd->htk", grad_rows, value_rows, preferred_element_type=jnp.float32
    )
    centre = jnp.sum(weights * grad_weights, axis=-1, keepdims=True)
    grad_scores = (weights * (grad_weights - centre) * scale).astype(jnp.bfloat16)
    grad_queries = jnp.einsum(
        "htk,khd->thd", grad_scores, key_rows, preferred_element_type=jnp.float32
    ).reshape(rows, -1)
    key_terms = jnp.einsum("htk,thd->khd", grad_scores, queries, preferred_element_type=jnp.float32)
    value_terms = jnp.einsum("htk,thd->khd", rounded, grad_rows, preferred_element_type=jnp.float32)
    input_grad = (grads.astype(jnp.float32) + grad_queries).astype(jnp.bfloat16)
    key_count = key_rows.shape[0]
    return (
        input_grad,
        key_terms.reshape(key_count, -1).astype(jnp.bfloat16),
        value_terms.reshape(key_count, -1).astype(jnp.bfloat16),
    )


def routed(stream_in, saved_in, grad_out, mem_keys, mem_values, owner_map, block_ids):
    replicas = lax.axis_size("dp")
    local_blocks = mem_keys.shape[1]
    block_rows = mem_keys.shape[2]
    width = stream_in.shape[2]
    table_size = owner_map.shape[0]
    requested = block_ids.reshape(-1)
    picks = requested.shape[0]
    half = picks // 2
    matches = requested[:, None] == jnp.arange(table_size, dtype=jnp.int32)[None, :]
    places = jnp.sum(jnp.where(matches, owner_map[None, :], 0), axis=1)
    owners = places // local_blocks
    slot_ids = places % local_blocks
    owner_hits = owners[:, None] == jnp.arange(replicas, dtype=jnp.int32)[None, :]
    served = None
    wanted = jnp.sum(jnp.where(owner_hits, slot_ids[:, None], 0), axis=0)
    served = lax.all_to_all(
        wanted.reshape(replicas, 1), "dp", split_axis=0, concat_axis=0, tiled=True
    ).reshape(replicas)
    out_keys = jnp.take(mem_keys[0], served, axis=0)
    out_values = jnp.take(mem_values[0], served, axis=0)
    got_keys, got_values = (
        lax.all_to_all(out_keys, "dp", split_axis=0, concat_axis=0, tiled=True),
        lax.all_to_all(out_values, "dp", split_axis=0, concat_axis=0, tiled=True),
    )
    fetched_keys = jnp.take(got_keys, owners, axis=0)
    fetched_values = jnp.take(got_values, owners, axis=0)
    forward_keys = fetched_keys[:half].reshape(-1, width)
    forward_values = fetched_values[:half].reshape(-1, width)
    backward_keys = fetched_keys[half:].reshape(-1, width)
    backward_values = fetched_values[half:].reshape(-1, width)
    attended = forward_part(stream_in[0], forward_keys, forward_values)[5]
    section_out = (stream_in[0].astype(jnp.float32) + attended).astype(jnp.bfloat16)
    next_input = from_behind(section_out[None], "pipe", 1)
    input_grad, key_terms, value_terms = backward_part(
        saved_in[0], grad_out[0], backward_keys, backward_values
    )
    grad_back = from_behind(input_grad[None], "pipe", -1)
    key_blocks = key_terms.reshape(half, block_rows, width)
    value_blocks = value_terms.reshape(half, block_rows, width)
    back_hits = owner_hits[half:].astype(jnp.bfloat16)
    send_keys = jnp.einsum(
        "ro,rtf->otf", back_hits, key_blocks, preferred_element_type=jnp.float32
    ).astype(jnp.bfloat16)
    send_values = jnp.einsum(
        "ro,rtf->otf", back_hits, value_blocks, preferred_element_type=jnp.float32
    ).astype(jnp.bfloat16)
    recv_keys, recv_values = (
        lax.all_to_all(send_keys, "dp", split_axis=0, concat_axis=0, tiled=True),
        lax.all_to_all(send_values, "dp", split_axis=0, concat_axis=0, tiled=True),
    )
    slot_hits = (served[:, None] == jnp.arange(local_blocks, dtype=jnp.int32)[None, :]).astype(
        jnp.bfloat16
    )
    key_grad = jnp.einsum(
        "sm,stf->mtf", slot_hits, recv_keys, preferred_element_type=jnp.float32
    ).astype(jnp.bfloat16)
    value_grad = jnp.einsum(
        "sm,stf->mtf", slot_hits, recv_values, preferred_element_type=jnp.float32
    ).astype(jnp.bfloat16)
    return (next_input, grad_back, key_grad[None], value_grad[None])


def local(*args):
    replicas, (_, tokens, width) = lax.axis_size("dp"), args[0].shape
    few = replicas <= DIRECT_REPLICAS
    one_each = args[-1].size == 2 and lax.axis_size("pipe") == 2 and width % tokens == 0
    small = args[-2].size <= 256
    return (direct if few and one_each and small else routed)(*args)


def solution(mesh):
    in_specs = (
        P("pipe", "dp", "tensor"),
        P("pipe", "dp", "tensor"),
        P("pipe", "dp", "tensor"),
        P("pipe", "dp", None, "tensor"),
        P("pipe", "dp", None, "tensor"),
        P(),
        P(None, "pipe", "dp", None),
    )
    out_specs = (
        P("pipe", "dp", "tensor"),
        P("pipe", "dp", "tensor"),
        P("pipe", "dp", None, "tensor"),
        P("pipe", "dp", None, "tensor"),
    )
    return jax.shard_map(local, mesh=mesh, in_specs=in_specs, out_specs=out_specs, check_vma=False)
```

```python
import functools
import math

import jax
import jax.numpy as jnp
from jax import lax
from jax.experimental import pallas as pl
from jax.experimental.pallas import tpu as pltpu
from jax.sharding import PartitionSpec as P

HEAD_DIM = 128
DIRECT_REPLICAS = 8
HBM = pl.BlockSpec(memory_space=pltpu.HBM)
VMEM = pl.BlockSpec(memory_space=pltpu.VMEM)
SMEM = pl.BlockSpec(memory_space=pltpu.SMEM)
NT = (((1,), (1,)), ((), ()))
NN = (((1,), (0,)), ((), ()))
TN = (((0,), (0,)), ((), ()))


def padded(rows):
    return -(-rows // 16) * 16


def dot(a, b, dims):
    return lax.dot_general(a, b, dims, preferred_element_type=jnp.float32)


def by_head(block):
    keys, width = block.shape
    heads = width // HEAD_DIM
    wide = jnp.broadcast_to(block.astype(jnp.float32)[None], (heads, keys, width))
    head = lax.broadcasted_iota(jnp.int32, wide.shape, 0)
    feature_head = lax.broadcasted_iota(jnp.int32, wide.shape, 2) // HEAD_DIM
    return jnp.where(head == feature_head, wide, 0.0).reshape(heads * keys, width).astype(block.dtype)


def groups(width):
    step = min(width, 2 * HEAD_DIM)
    return [slice(i, i + step) for i in range(0, width, step)]


def per_head(block, rows):
    parts = [dot(by_head(block[:, at]), rows[:, at], NT) for at in groups(rows.shape[1])]
    return jnp.concatenate(parts, axis=0).reshape(-1, block.shape[0], rows.shape[0])


def reduced(by_key, rows):
    keys, tokens = by_key.shape[1:]
    parts = []
    for at in groups(rows.shape[1]):
        heads = slice(at.start // HEAD_DIM, at.stop // HEAD_DIM)
        product = dot(by_key[heads].reshape(-1, tokens), rows[:, at], NN)
        parts += [
            product[h * keys : (h + 1) * keys, h * HEAD_DIM : (h + 1) * HEAD_DIM]
            for h in range(heads.stop - heads.start)
        ]
    return jnp.concatenate(parts, axis=1)


def softmax_t(keys, rows):
    scores = per_head(keys, rows) * (1.0 / math.sqrt(HEAD_DIM))
    exponent = jnp.exp(scores - jnp.max(scores, axis=1, keepdims=True))
    return exponent / jnp.sum(exponent, axis=1, keepdims=True)


def pick(refs, first, behind, slot):
    block = refs[0][first + slot]
    for i in range(1, len(refs)):
        block = jnp.where(behind == len(refs) - i, refs[i][first + slot], block)
    return block


def stack_kernel(keys_ref, values_ref, out_ref, sems):
    slots = keys_ref.shape[0]
    copies = []
    for i in range(slots):
        copies.append(pltpu.make_async_copy(keys_ref.at[i], out_ref.at[i], sems.at[i]))
        copies.append(pltpu.make_async_copy(values_ref.at[i], out_ref.at[slots + i], sems.at[slots + i]))
    for copy in copies:
        copy.start()
    for copy in copies:
        copy.wait()


def fetch_kernel(map_ref, ids_ref, stream_ref, saved_ref, grad_ref, *refs):
    saved_near, grad_near, sent_ref, place_ref, map_near, ids_near, sems = refs
    rows = sent_ref.at[: stream_ref.shape[0]]
    section = lax.axis_index("pipe")
    small = [
        pltpu.make_async_copy(map_ref, map_near, sems.at[0]),
        pltpu.make_async_copy(ids_ref, ids_near, sems.at[1]),
    ]
    large = [
        pltpu.make_async_copy(saved_ref, saved_near, sems.at[2]),
        pltpu.make_async_copy(grad_ref, grad_near, sems.at[3]),
    ]
    for copy in small + large:
        copy.start()

    @pl.when(section == 0)
    def _():
        pltpu.make_async_copy(stream_ref, rows, sems.at[4]).start()

    @pl.when(section != 0)
    def _():
        pltpu.make_async_copy(grad_ref, rows, sems.at[4]).start()

    for copy in small:
        copy.wait()
    for i in range(place_ref.shape[0]):
        place_ref[i] = map_near[ids_near[i]]
    for copy in large:
        copy.wait()
    pltpu.make_async_copy(grad_ref, rows, sems.at[4]).wait()


def score_kernel(slots, place_ref, saved_ref, grad_ref, rows_ref, *refs):
    memory, (terms_ref, sent_ref) = refs[:-2], refs[-2:]
    me = lax.axis_index("dp")
    section = lax.axis_index("pipe")
    tokens, width = saved_ref.shape
    heads = width // HEAD_DIM
    back = place_ref[1]
    behind, slot = lax.rem(me - back // slots + len(memory), len(memory)), back % slots
    keys = pick(memory, 0, behind, slot)
    values = pick(memory, slots, behind, slot)
    count = keys.shape[0]
    first, second = tokens, tokens + padded(count)

    @pl.when(section == 0)
    def _():
        ahead = place_ref[0]
        behind, slot = lax.rem(me - ahead // slots + len(memory), len(memory)), ahead % slots
        sent_ref[first : first + count, :] = pick(memory, 0, behind, slot)
        sent_ref[second : second + count, :] = pick(memory, slots, behind, slot)

    saved, grads = saved_ref[...], grad_ref[...]
    weights = softmax_t(keys, saved)
    grad_weights = per_head(values, grads)
    centre = jnp.sum(weights * grad_weights, axis=1, keepdims=True)
    grad_scores = weights * (grad_weights - centre) * (1.0 / math.sqrt(HEAD_DIM))
    flat = heads * count
    grad_scores = grad_scores.astype(jnp.bfloat16)
    terms_ref[:, :width] = reduced(grad_scores, saved).astype(jnp.bfloat16)
    terms_ref[:, width : 2 * width] = reduced(weights.astype(jnp.bfloat16), grads).astype(jnp.bfloat16)
    grad_scores = grad_scores.reshape(flat, tokens)
    place = jnp.full((count, HEAD_DIM), back, jnp.int32)
    terms_ref[:, 2 * width :] = place.astype(jnp.float32).astype(jnp.bfloat16)
    @pl.when(section != 0)
    def _():
        sent_ref[first : first + count, :] = keys
        part = flat * tokens // width
        for i in range(width // tokens):
            at = slice(i * tokens, (i + 1) * tokens)
            sent_ref[second : second + part, at] = grad_scores[i * part : (i + 1) * part, :]


def output_kernel(tokens, count, sent_ref, next_ref, back_ref):
    width = sent_ref.shape[1]
    heads = width // HEAD_DIM
    first, second = tokens, tokens + padded(count)
    keys = sent_ref[first : first + count, :]
    rows = sent_ref[:tokens, :]
    section = lax.axis_index("pipe")

    @pl.when(section == 0)
    def _():
        next_ref[...] = jnp.zeros_like(next_ref)
        part = heads * count * tokens // width
        grad_scores = [
            sent_ref[second : second + part, i * tokens : (i + 1) * tokens]
            for i in range(width // tokens)
        ]
        added = dot(jnp.concatenate(grad_scores, axis=0), by_head(keys), TN)
        back_ref[...] = (rows.astype(jnp.float32) + added).astype(jnp.bfloat16)

    @pl.when(section != 0)
    def _():
        back_ref[...] = jnp.zeros_like(back_ref)
        values = by_head(sent_ref[second : second + count, :])
        weights = softmax_t(keys, rows).astype(jnp.bfloat16).reshape(-1, tokens)
        added = dot(weights, values, TN)
        next_ref[...] = (rows.astype(jnp.float32) + added).astype(jnp.bfloat16)


def sum_kernel(slots, *refs):
    terms_refs, (key_ref, value_ref) = refs[:-2], refs[-2:]
    me = lax.axis_index("dp")
    width = key_ref.shape[2]
    tiles = width // HEAD_DIM
    terms = [ref[...].astype(jnp.float32) for ref in terms_refs]
    for slot in range(slots):
        here = (me * slots + slot).astype(jnp.float32)
        hits = [t[:, 2 * width :] == here for t in terms]
        for i in range(2 * tiles):
            at = slice(i * HEAD_DIM, (i + 1) * HEAD_DIM)
            total = sum(jnp.where(hit, t[:, at], 0.0) for hit, t in zip(hits, terms))
            out, j = (key_ref, i) if i < tiles else (value_ref, i - tiles)
            out[slot, :, j * HEAD_DIM : (j + 1) * HEAD_DIM] = total.astype(jnp.bfloat16)


def exchange(x, replicas):
    return [x] + [
        lax.ppermute(x, "dp", [(i, (i + d) % replicas) for i in range(replicas)])
        for d in range(replicas - 1, 0, -1)
    ]


def vmem(x):
    return pltpu.with_memory_space_constraint(x, pltpu.VMEM)


def hbm(x):
    return pltpu.with_memory_space_constraint(x, pltpu.HBM)


def smem(x):
    return pltpu.with_memory_space_constraint(x, pltpu.SMEM)


def call(kernel, name, out, in_specs, scratch=(), moved=0, aliases=()):
    return pl.pallas_call(
        kernel,
        out_shape=out,
        in_specs=in_specs,
        out_specs=jax.tree.map(lambda o: SMEM if o.shape == (2,) else VMEM, out),
        scratch_shapes=scratch,
        input_output_aliases=dict(aliases),
        compiler_params=pltpu.CompilerParams(vmem_limit_bytes=16 * 1024 * 1024),
        cost_estimate=pl.CostEstimate(flops=0, bytes_accessed=moved, transcendentals=0),
        name=name,
    )


def direct(stream_in, saved_in, grad_out, mem_keys, mem_values, owner_map, block_ids):
    replicas = lax.axis_size("dp")
    slots, block_rows, width = mem_keys.shape[1:]
    tokens = stream_in.shape[1]
    rows = pltpu.VMEM((tokens, width), jnp.bfloat16)
    grad_lines = width // HEAD_DIM * block_rows * tokens // width
    sent_rows = tokens + padded(block_rows) + padded(max(block_rows, grad_lines))
    sent = pltpu.VMEM((sent_rows, width), jnp.bfloat16)
    stacked = call(
        stack_kernel,
        "stack",
        pltpu.VMEM((2 * slots, block_rows, width), jnp.bfloat16),
        [HBM] * 2,
        [pltpu.SemaphoreType.DMA((2 * slots,))],
    )(hbm(mem_keys[0]), hbm(mem_values[0]))
    stacked, *own = lax.optimization_barrier(
        (stacked, owner_map, block_ids.reshape(-1), stream_in[0], saved_in[0], grad_out[0])
    )
    memory = exchange(stacked, replicas)
    saved, grads, to_send, places = call(
        fetch_kernel,
        "fetch",
        (rows, rows, sent, pltpu.SMEM((2,), jnp.int32)),
        [HBM] * 5,
        [
            pltpu.SMEM(owner_map.shape, jnp.int32),
            pltpu.SMEM((2,), jnp.int32),
            pltpu.SemaphoreType.DMA((5,)),
        ],
        12 * tokens * width,
    )(*map(hbm, own))
    terms, to_send = call(
        functools.partial(score_kernel, slots),
        "scores",
        (pltpu.VMEM((block_rows, 2 * width + HEAD_DIM), jnp.bfloat16), sent),
        [SMEM] + [VMEM] * (3 + replicas),
        aliases={3: 1}.items(),
    )(smem(places), *map(vmem, (saved, grads, to_send, *memory)))
    other_sent = lax.ppermute(to_send, "pipe", [(0, 1), (1, 0)])
    term_parts = exchange(terms, replicas)
    next_input, grad_back = call(
        functools.partial(output_kernel, tokens, block_rows),
        "outputs",
        (jax.ShapeDtypeStruct((tokens, width), jnp.bfloat16),) * 2,
        [VMEM],
        (),
        4 * tokens * width,
    )(vmem(other_sent))
    *term_parts, next_input, grad_back = lax.optimization_barrier((*term_parts, next_input, grad_back))
    key_grad, value_grad = call(
        functools.partial(sum_kernel, slots),
        "sums",
        (jax.ShapeDtypeStruct((slots, block_rows, width), jnp.bfloat16),) * 2,
        [VMEM] * replicas,
    )(*map(vmem, term_parts))
    return next_input[None], grad_back[None], key_grad[None], value_grad[None]


def from_behind(x, axis, by):
    peers = lax.axis_size(axis)
    pairs = [(i, i + by) for i in range(peers) if 0 <= i + by < peers]
    return lax.ppermute(x, axis, pairs)


def forward_part(inputs, memory_keys, memory_values):
    rows = inputs.shape[0]
    heads_count = inputs.shape[1] // HEAD_DIM
    scale = 1.0 / math.sqrt(HEAD_DIM)
    queries = inputs.reshape(rows, heads_count, HEAD_DIM)
    key_rows = memory_keys.reshape(-1, heads_count, HEAD_DIM)
    value_rows = memory_values.reshape(-1, heads_count, HEAD_DIM)
    scores = (
        jnp.einsum("thd,khd->htk", queries, key_rows, preferred_element_type=jnp.float32) * scale
    )
    exponent = jnp.exp(scores - jnp.max(scores, axis=-1, keepdims=True))
    weights = exponent / jnp.sum(exponent, axis=-1, keepdims=True)
    rounded = weights.astype(jnp.bfloat16)
    attended = jnp.einsum(
        "htk,khd->thd", rounded, value_rows, preferred_element_type=jnp.float32
    ).reshape(rows, -1)
    return (queries, key_rows, value_rows, weights, rounded, attended)


def backward_part(inputs, grads, memory_keys, memory_values):
    queries, key_rows, value_rows, weights, rounded, attended = forward_part(
        inputs, memory_keys, memory_values
    )
    rows = inputs.shape[0]
    heads_count = queries.shape[1]
    scale = 1.0 / math.sqrt(HEAD_DIM)
    grad_rows = grads.reshape(rows, heads_count, HEAD_DIM)
    grad_weights = jnp.einsum(
        "thd,khd->htk", grad_rows, value_rows, preferred_element_type=jnp.float32
    )
    centre = jnp.sum(weights * grad_weights, axis=-1, keepdims=True)
    grad_scores = (weights * (grad_weights - centre) * scale).astype(jnp.bfloat16)
    grad_queries = jnp.einsum(
        "htk,khd->thd", grad_scores, key_rows, preferred_element_type=jnp.float32
    ).reshape(rows, -1)
    key_terms = jnp.einsum("htk,thd->khd", grad_scores, queries, preferred_element_type=jnp.float32)
    value_terms = jnp.einsum("htk,thd->khd", rounded, grad_rows, preferred_element_type=jnp.float32)
    input_grad = (grads.astype(jnp.float32) + grad_queries).astype(jnp.bfloat16)
    key_count = key_rows.shape[0]
    return (
        input_grad,
        key_terms.reshape(key_count, -1).astype(jnp.bfloat16),
        value_terms.reshape(key_count, -1).astype(jnp.bfloat16),
    )


def routed(stream_in, saved_in, grad_out, mem_keys, mem_values, owner_map, block_ids):
    replicas = lax.axis_size("dp")
    local_blocks = mem_keys.shape[1]
    block_rows = mem_keys.shape[2]
    width = stream_in.shape[2]
    table_size = owner_map.shape[0]
    requested = block_ids.reshape(-1)
    picks = requested.shape[0]
    half = picks // 2
    matches = requested[:, None] == jnp.arange(table_size, dtype=jnp.int32)[None, :]
    places = jnp.sum(jnp.where(matches, owner_map[None, :], 0), axis=1)
    owners = places // local_blocks
    slot_ids = places % local_blocks
    owner_hits = owners[:, None] == jnp.arange(replicas, dtype=jnp.int32)[None, :]
    served = None
    wanted = jnp.sum(jnp.where(owner_hits, slot_ids[:, None], 0), axis=0)
    served = lax.all_to_all(
        wanted.reshape(replicas, 1), "dp", split_axis=0, concat_axis=0, tiled=True
    ).reshape(replicas)
    out_keys = jnp.take(mem_keys[0], served, axis=0)
    out_values = jnp.take(mem_values[0], served, axis=0)
    got_keys, got_values = (
        lax.all_to_all(out_keys, "dp", split_axis=0, concat_axis=0, tiled=True),
        lax.all_to_all(out_values, "dp", split_axis=0, concat_axis=0, tiled=True),
    )
    fetched_keys = jnp.take(got_keys, owners, axis=0)
    fetched_values = jnp.take(got_values, owners, axis=0)
    forward_keys = fetched_keys[:half].reshape(-1, width)
    forward_values = fetched_values[:half].reshape(-1, width)
    backward_keys = fetched_keys[half:].reshape(-1, width)
    backward_values = fetched_values[half:].reshape(-1, width)
    attended = forward_part(stream_in[0], forward_keys, forward_values)[5]
    section_out = (stream_in[0].astype(jnp.float32) + attended).astype(jnp.bfloat16)
    next_input = from_behind(section_out[None], "pipe", 1)
    input_grad, key_terms, value_terms = backward_part(
        saved_in[0], grad_out[0], backward_keys, backward_values
    )
    grad_back = from_behind(input_grad[None], "pipe", -1)
    key_blocks = key_terms.reshape(half, block_rows, width)
    value_blocks = value_terms.reshape(half, block_rows, width)
    back_hits = owner_hits[half:].astype(jnp.bfloat16)
    send_keys = jnp.einsum(
        "ro,rtf->otf", back_hits, key_blocks, preferred_element_type=jnp.float32
    ).astype(jnp.bfloat16)
    send_values = jnp.einsum(
        "ro,rtf->otf", back_hits, value_blocks, preferred_element_type=jnp.float32
    ).astype(jnp.bfloat16)
    recv_keys, recv_values = (
        lax.all_to_all(send_keys, "dp", split_axis=0, concat_axis=0, tiled=True),
        lax.all_to_all(send_values, "dp", split_axis=0, concat_axis=0, tiled=True),
    )
    slot_hits = (served[:, None] == jnp.arange(local_blocks, dtype=jnp.int32)[None, :]).astype(
        jnp.bfloat16
    )
    key_grad = jnp.einsum(
        "sm,stf->mtf", slot_hits, recv_keys, preferred_element_type=jnp.float32
    ).astype(jnp.bfloat16)
    value_grad = jnp.einsum(
        "sm,stf->mtf", slot_hits, recv_values, preferred_element_type=jnp.float32
    ).astype(jnp.bfloat16)
    return (next_input, grad_back, key_grad[None], value_grad[None])


def local(*args):
    replicas, (_, tokens, width) = lax.axis_size("dp"), args[0].shape
    few = replicas <= DIRECT_REPLICAS
    one_each = args[-1].size == 2 and lax.axis_size("pipe") == 2 and width % tokens == 0
    small = args[-2].size <= 256
    return (direct if few and one_each and small else routed)(*args)


def solution(mesh):
    in_specs = (
        P("pipe", "dp", "tensor"),
        P("pipe", "dp", "tensor"),
        P("pipe", "dp", "tensor"),
        P("pipe", "dp", None, "tensor"),
        P("pipe", "dp", None, "tensor"),
        P(),
        P(None, "pipe", "dp", None),
    )
    out_specs = (
        P("pipe", "dp", "tensor"),
        P("pipe", "dp", "tensor"),
        P("pipe", "dp", None, "tensor"),
        P("pipe", "dp", None, "tensor"),
    )
    return jax.shard_map(local, mesh=mesh, in_specs=in_specs, out_specs=out_specs, check_vma=False)
```

```python
import functools
import math

import jax
import jax.numpy as jnp
from jax import lax
from jax.experimental import pallas as pl
from jax.experimental.pallas import tpu as pltpu
from jax.sharding import PartitionSpec as P

HEAD_DIM = 128
DIRECT_REPLICAS = 8
SEND = ((2, 0, 3, 1), (3, 2, 1, 0), (1, 3, 0, 2))
HBM = pl.BlockSpec(memory_space=pltpu.HBM)
VMEM = pl.BlockSpec(memory_space=pltpu.VMEM)
SMEM = pl.BlockSpec(memory_space=pltpu.SMEM)
NT = (((1,), (1,)), ((), ()))
NN = (((1,), (0,)), ((), ()))
TN = (((0,), (0,)), ((), ()))


def padded(rows):
    return -(-rows // 16) * 16


def dot(a, b, dims):
    return lax.dot_general(a, b, dims, preferred_element_type=jnp.float32)


def by_head(block):
    keys, width = block.shape
    heads = width // HEAD_DIM
    wide = jnp.broadcast_to(block.astype(jnp.float32)[None], (heads, keys, width))
    head = lax.broadcasted_iota(jnp.int32, wide.shape, 0)
    feature_head = lax.broadcasted_iota(jnp.int32, wide.shape, 2) // HEAD_DIM
    return jnp.where(head == feature_head, wide, 0.0).reshape(heads * keys, width).astype(block.dtype)


def groups(width):
    step = min(width, 2 * HEAD_DIM)
    return [slice(i, i + step) for i in range(0, width, step)]


def per_head(block, rows):
    parts = [dot(by_head(block[:, at]), rows[:, at], NT) for at in groups(rows.shape[1])]
    return jnp.concatenate(parts, axis=0).reshape(-1, block.shape[0], rows.shape[0])


def reduced(by_key, rows):
    keys, tokens = by_key.shape[1:]
    parts = []
    for at in groups(rows.shape[1]):
        heads = slice(at.start // HEAD_DIM, at.stop // HEAD_DIM)
        product = dot(by_key[heads].reshape(-1, tokens), rows[:, at], NN)
        parts += [
            product[h * keys : (h + 1) * keys, h * HEAD_DIM : (h + 1) * HEAD_DIM]
            for h in range(heads.stop - heads.start)
        ]
    return jnp.concatenate(parts, axis=1)


def softmax_t(keys, rows):
    scores = per_head(keys, rows) * (1.0 / math.sqrt(HEAD_DIM))
    exponent = jnp.exp(scores - jnp.max(scores, axis=1, keepdims=True))
    return exponent / jnp.sum(exponent, axis=1, keepdims=True)


def pick(refs, first, behind, slot):
    block = refs[0][first + slot]
    for i in range(1, len(refs)):
        block = jnp.where(behind == len(refs) - i, refs[i][first + slot], block)
    return block


def stack_kernel(keys_ref, values_ref, out_ref, sems):
    slots = keys_ref.shape[0]
    copies = []
    for i in range(slots):
        copies.append(pltpu.make_async_copy(keys_ref.at[i], out_ref.at[i], sems.at[i]))
        copies.append(pltpu.make_async_copy(values_ref.at[i], out_ref.at[slots + i], sems.at[slots + i]))
    for copy in copies:
        copy.start()
    for copy in copies:
        copy.wait()


def fetch_kernel(map_ref, ids_ref, stream_ref, saved_ref, grad_ref, *refs):
    saved_near, grad_near, sent_ref, place_ref, map_near, ids_near, sems = refs
    rows = sent_ref.at[: stream_ref.shape[0]]
    section = lax.axis_index("pipe")
    small = [
        pltpu.make_async_copy(map_ref, map_near, sems.at[0]),
        pltpu.make_async_copy(ids_ref, ids_near, sems.at[1]),
    ]
    large = [
        pltpu.make_async_copy(saved_ref, saved_near, sems.at[2]),
        pltpu.make_async_copy(grad_ref, grad_near, sems.at[3]),
    ]
    for copy in small + large:
        copy.start()

    @pl.when(section == 0)
    def _():
        pltpu.make_async_copy(stream_ref, rows, sems.at[4]).start()

    @pl.when(section != 0)
    def _():
        pltpu.make_async_copy(grad_ref, rows, sems.at[4]).start()

    for copy in small:
        copy.wait()
    for i in range(place_ref.shape[0]):
        place_ref[i] = map_near[ids_near[i]]
    for copy in large:
        copy.wait()
    pltpu.make_async_copy(grad_ref, rows, sems.at[4]).wait()


def score_kernel(slots, place_ref, saved_ref, grad_ref, rows_ref, *refs):
    memory, (terms_ref, sent_ref) = refs[:-2], refs[-2:]
    me = lax.axis_index("dp")
    section = lax.axis_index("pipe")
    tokens, width = saved_ref.shape
    heads = width // HEAD_DIM
    back = place_ref[1]
    behind, slot = lax.rem(me - back // slots + len(memory), len(memory)), back % slots
    keys = pick(memory, 0, behind, slot)
    values = pick(memory, slots, behind, slot)
    count = keys.shape[0]
    first, second = tokens, tokens + padded(count)

    @pl.when(section == 0)
    def _():
        ahead = place_ref[0]
        behind, slot = lax.rem(me - ahead // slots + len(memory), len(memory)), ahead % slots
        sent_ref[first : first + count, :] = pick(memory, 0, behind, slot)
        sent_ref[second : second + count, :] = pick(memory, slots, behind, slot)

    saved, grads = saved_ref[...], grad_ref[...]
    weights = softmax_t(keys, saved)
    grad_weights = per_head(values, grads)
    centre = jnp.sum(weights * grad_weights, axis=1, keepdims=True)
    grad_scores = weights * (grad_weights - centre) * (1.0 / math.sqrt(HEAD_DIM))
    flat = heads * count
    grad_scores = grad_scores.astype(jnp.bfloat16)
    terms_ref[:, :width] = reduced(grad_scores, saved).astype(jnp.bfloat16)
    terms_ref[:, width : 2 * width] = reduced(weights.astype(jnp.bfloat16), grads).astype(jnp.bfloat16)
    grad_scores = grad_scores.reshape(flat, tokens)
    place = jnp.full((count, HEAD_DIM), back, jnp.int32)
    terms_ref[:, 2 * width :] = place.astype(jnp.float32).astype(jnp.bfloat16)
    @pl.when(section != 0)
    def _():
        sent_ref[first : first + count, :] = keys
        part = flat * tokens // width
        for i in range(width // tokens):
            at = slice(i * tokens, (i + 1) * tokens)
            sent_ref[second : second + part, at] = grad_scores[i * part : (i + 1) * part, :]


def output_kernel(tokens, count, sent_ref, next_ref, back_ref):
    width = sent_ref.shape[1]
    heads = width // HEAD_DIM
    first, second = tokens, tokens + padded(count)
    keys = sent_ref[first : first + count, :]
    rows = sent_ref[:tokens, :]
    section = lax.axis_index("pipe")

    @pl.when(section == 0)
    def _():
        next_ref[...] = jnp.zeros_like(next_ref)
        part = heads * count * tokens // width
        grad_scores = [
            sent_ref[second : second + part, i * tokens : (i + 1) * tokens]
            for i in range(width // tokens)
        ]
        added = dot(jnp.concatenate(grad_scores, axis=0), by_head(keys), TN)
        back_ref[...] = (rows.astype(jnp.float32) + added).astype(jnp.bfloat16)

    @pl.when(section != 0)
    def _():
        back_ref[...] = jnp.zeros_like(back_ref)
        values = by_head(sent_ref[second : second + count, :])
        weights = softmax_t(keys, rows).astype(jnp.bfloat16).reshape(-1, tokens)
        added = dot(weights, values, TN)
        next_ref[...] = (rows.astype(jnp.float32) + added).astype(jnp.bfloat16)


def sum_kernel(slots, *refs):
    terms_refs, (key_ref, value_ref) = refs[:-2], refs[-2:]
    me = lax.axis_index("dp")
    width = key_ref.shape[2]
    tiles = width // HEAD_DIM
    terms = [ref[...].astype(jnp.float32) for ref in terms_refs]
    for slot in range(slots):
        here = (me * slots + slot).astype(jnp.float32)
        hits = [t[:, 2 * width :] == here for t in terms]
        for i in range(2 * tiles):
            at = slice(i * HEAD_DIM, (i + 1) * HEAD_DIM)
            total = sum(jnp.where(hit, t[:, at], 0.0) for hit, t in zip(hits, terms))
            out, j = (key_ref, i) if i < tiles else (value_ref, i - tiles)
            out[slot, :, j * HEAD_DIM : (j + 1) * HEAD_DIM] = total.astype(jnp.bfloat16)


def exchange(x, replicas, patterns=None):
    shifts = [[(i + d) % replicas for i in range(replicas)] for d in range(replicas - 1, 0, -1)]
    return [x] + [lax.ppermute(x, "dp", list(enumerate(p))) for p in patterns or shifts]


def vmem(x):
    return pltpu.with_memory_space_constraint(x, pltpu.VMEM)


def hbm(x):
    return pltpu.with_memory_space_constraint(x, pltpu.HBM)


def smem(x):
    return pltpu.with_memory_space_constraint(x, pltpu.SMEM)


def call(kernel, name, out, in_specs, scratch=(), moved=0, aliases=()):
    return pl.pallas_call(
        kernel,
        out_shape=out,
        in_specs=in_specs,
        out_specs=jax.tree.map(lambda o: SMEM if o.shape == (2,) else VMEM, out),
        scratch_shapes=scratch,
        input_output_aliases=dict(aliases),
        compiler_params=pltpu.CompilerParams(vmem_limit_bytes=16 * 1024 * 1024),
        cost_estimate=pl.CostEstimate(flops=0, bytes_accessed=moved, transcendentals=0),
        name=name,
    )


def direct(stream_in, saved_in, grad_out, mem_keys, mem_values, owner_map, block_ids):
    replicas = lax.axis_size("dp")
    slots, block_rows, width = mem_keys.shape[1:]
    tokens = stream_in.shape[1]
    rows = pltpu.VMEM((tokens, width), jnp.bfloat16)
    grad_lines = width // HEAD_DIM * block_rows * tokens // width
    sent_rows = tokens + padded(block_rows) + padded(max(block_rows, grad_lines))
    sent = pltpu.VMEM((sent_rows, width), jnp.bfloat16)
    stacked = call(
        stack_kernel,
        "stack",
        pltpu.VMEM((2 * slots, block_rows, width), jnp.bfloat16),
        [HBM] * 2,
        [pltpu.SemaphoreType.DMA((2 * slots,))],
    )(hbm(mem_keys[0]), hbm(mem_values[0]))
    stacked, *own = lax.optimization_barrier(
        (stacked, owner_map, block_ids.reshape(-1), stream_in[0], saved_in[0], grad_out[0])
    )
    memory = exchange(stacked, replicas)
    saved, grads, to_send, places = call(
        fetch_kernel,
        "fetch",
        (rows, rows, sent, pltpu.SMEM((2,), jnp.int32)),
        [HBM] * 5,
        [
            pltpu.SMEM(owner_map.shape, jnp.int32),
            pltpu.SMEM((2,), jnp.int32),
            pltpu.SemaphoreType.DMA((5,)),
        ],
        12 * tokens * width,
    )(*map(hbm, own))
    terms, to_send = call(
        functools.partial(score_kernel, slots),
        "scores",
        (pltpu.VMEM((block_rows, 2 * width + HEAD_DIM), jnp.bfloat16), sent),
        [SMEM] + [VMEM] * (3 + replicas),
        aliases={3: 1}.items(),
    )(smem(places), *map(vmem, (saved, grads, to_send, *memory)))
    other_sent = lax.ppermute(to_send, "pipe", [(0, 1), (1, 0)])
    term_parts = exchange(terms, replicas, SEND if replicas == 4 else None)
    next_input, grad_back = call(
        functools.partial(output_kernel, tokens, block_rows),
        "outputs",
        (jax.ShapeDtypeStruct((tokens, width), jnp.bfloat16),) * 2,
        [VMEM],
        (),
        4 * tokens * width,
    )(vmem(other_sent))
    *term_parts, next_input, grad_back = lax.optimization_barrier((*term_parts, next_input, grad_back))
    key_grad, value_grad = call(
        functools.partial(sum_kernel, slots),
        "sums",
        (jax.ShapeDtypeStruct((slots, block_rows, width), jnp.bfloat16),) * 2,
        [VMEM] * replicas,
    )(*map(vmem, term_parts))
    return next_input[None], grad_back[None], key_grad[None], value_grad[None]


def from_behind(x, axis, by):
    peers = lax.axis_size(axis)
    pairs = [(i, i + by) for i in range(peers) if 0 <= i + by < peers]
    return lax.ppermute(x, axis, pairs)


def forward_part(inputs, memory_keys, memory_values):
    rows = inputs.shape[0]
    heads_count = inputs.shape[1] // HEAD_DIM
    scale = 1.0 / math.sqrt(HEAD_DIM)
    queries = inputs.reshape(rows, heads_count, HEAD_DIM)
    key_rows = memory_keys.reshape(-1, heads_count, HEAD_DIM)
    value_rows = memory_values.reshape(-1, heads_count, HEAD_DIM)
    scores = (
        jnp.einsum("thd,khd->htk", queries, key_rows, preferred_element_type=jnp.float32) * scale
    )
    exponent = jnp.exp(scores - jnp.max(scores, axis=-1, keepdims=True))
    weights = exponent / jnp.sum(exponent, axis=-1, keepdims=True)
    rounded = weights.astype(jnp.bfloat16)
    attended = jnp.einsum(
        "htk,khd->thd", rounded, value_rows, preferred_element_type=jnp.float32
    ).reshape(rows, -1)
    return (queries, key_rows, value_rows, weights, rounded, attended)


def backward_part(inputs, grads, memory_keys, memory_values):
    queries, key_rows, value_rows, weights, rounded, attended = forward_part(
        inputs, memory_keys, memory_values
    )
    rows = inputs.shape[0]
    heads_count = queries.shape[1]
    scale = 1.0 / math.sqrt(HEAD_DIM)
    grad_rows = grads.reshape(rows, heads_count, HEAD_DIM)
    grad_weights = jnp.einsum(
        "thd,khd->htk", grad_rows, value_rows, preferred_element_type=jnp.float32
    )
    centre = jnp.sum(weights * grad_weights, axis=-1, keepdims=True)
    grad_scores = (weights * (grad_weights - centre) * scale).astype(jnp.bfloat16)
    grad_queries = jnp.einsum(
        "htk,khd->thd", grad_scores, key_rows, preferred_element_type=jnp.float32
    ).reshape(rows, -1)
    key_terms = jnp.einsum("htk,thd->khd", grad_scores, queries, preferred_element_type=jnp.float32)
    value_terms = jnp.einsum("htk,thd->khd", rounded, grad_rows, preferred_element_type=jnp.float32)
    input_grad = (grads.astype(jnp.float32) + grad_queries).astype(jnp.bfloat16)
    key_count = key_rows.shape[0]
    return (
        input_grad,
        key_terms.reshape(key_count, -1).astype(jnp.bfloat16),
        value_terms.reshape(key_count, -1).astype(jnp.bfloat16),
    )


def routed(stream_in, saved_in, grad_out, mem_keys, mem_values, owner_map, block_ids):
    replicas = lax.axis_size("dp")
    local_blocks = mem_keys.shape[1]
    block_rows = mem_keys.shape[2]
    width = stream_in.shape[2]
    table_size = owner_map.shape[0]
    requested = block_ids.reshape(-1)
    picks = requested.shape[0]
    half = picks // 2
    matches = requested[:, None] == jnp.arange(table_size, dtype=jnp.int32)[None, :]
    places = jnp.sum(jnp.where(matches, owner_map[None, :], 0), axis=1)
    owners = places // local_blocks
    slot_ids = places % local_blocks
    owner_hits = owners[:, None] == jnp.arange(replicas, dtype=jnp.int32)[None, :]
    served = None
    wanted = jnp.sum(jnp.where(owner_hits, slot_ids[:, None], 0), axis=0)
    served = lax.all_to_all(
        wanted.reshape(replicas, 1), "dp", split_axis=0, concat_axis=0, tiled=True
    ).reshape(replicas)
    out_keys = jnp.take(mem_keys[0], served, axis=0)
    out_values = jnp.take(mem_values[0], served, axis=0)
    got_keys, got_values = (
        lax.all_to_all(out_keys, "dp", split_axis=0, concat_axis=0, tiled=True),
        lax.all_to_all(out_values, "dp", split_axis=0, concat_axis=0, tiled=True),
    )
    fetched_keys = jnp.take(got_keys, owners, axis=0)
    fetched_values = jnp.take(got_values, owners, axis=0)
    forward_keys = fetched_keys[:half].reshape(-1, width)
    forward_values = fetched_values[:half].reshape(-1, width)
    backward_keys = fetched_keys[half:].reshape(-1, width)
    backward_values = fetched_values[half:].reshape(-1, width)
    attended = forward_part(stream_in[0], forward_keys, forward_values)[5]
    section_out = (stream_in[0].astype(jnp.float32) + attended).astype(jnp.bfloat16)
    next_input = from_behind(section_out[None], "pipe", 1)
    input_grad, key_terms, value_terms = backward_part(
        saved_in[0], grad_out[0], backward_keys, backward_values
    )
    grad_back = from_behind(input_grad[None], "pipe", -1)
    key_blocks = key_terms.reshape(half, block_rows, width)
    value_blocks = value_terms.reshape(half, block_rows, width)
    back_hits = owner_hits[half:].astype(jnp.bfloat16)
    send_keys = jnp.einsum(
        "ro,rtf->otf", back_hits, key_blocks, preferred_element_type=jnp.float32
    ).astype(jnp.bfloat16)
    send_values = jnp.einsum(
        "ro,rtf->otf", back_hits, value_blocks, preferred_element_type=jnp.float32
    ).astype(jnp.bfloat16)
    recv_keys, recv_values = (
        lax.all_to_all(send_keys, "dp", split_axis=0, concat_axis=0, tiled=True),
        lax.all_to_all(send_values, "dp", split_axis=0, concat_axis=0, tiled=True),
    )
    slot_hits = (served[:, None] == jnp.arange(local_blocks, dtype=jnp.int32)[None, :]).astype(
        jnp.bfloat16
    )
    key_grad = jnp.einsum(
        "sm,stf->mtf", slot_hits, recv_keys, preferred_element_type=jnp.float32
    ).astype(jnp.bfloat16)
    value_grad = jnp.einsum(
        "sm,stf->mtf", slot_hits, recv_values, preferred_element_type=jnp.float32
    ).astype(jnp.bfloat16)
    return (next_input, grad_back, key_grad[None], value_grad[None])


def local(*args):
    replicas, (_, tokens, width) = lax.axis_size("dp"), args[0].shape
    few = replicas <= DIRECT_REPLICAS
    one_each = args[-1].size == 2 and lax.axis_size("pipe") == 2 and width % tokens == 0
    small = args[-2].size <= 256
    return (direct if few and one_each and small else routed)(*args)


def solution(mesh):
    in_specs = (
        P("pipe", "dp", "tensor"),
        P("pipe", "dp", "tensor"),
        P("pipe", "dp", "tensor"),
        P("pipe", "dp", None, "tensor"),
        P("pipe", "dp", None, "tensor"),
        P(),
        P(None, "pipe", "dp", None),
    )
    out_specs = (
        P("pipe", "dp", "tensor"),
        P("pipe", "dp", "tensor"),
        P("pipe", "dp", None, "tensor"),
        P("pipe", "dp", None, "tensor"),
    )
    return jax.shard_map(local, mesh=mesh, in_specs=in_specs, out_specs=out_specs, check_vma=False)
```
